32 devices in a mesh: section: 4 (over y, core), seq: 8 (over z, x).
Axes of the slice: x: 2, y: 2, z: 4, core: 2. Of those that a mesh axis runs over, the one named last changes fastest.
Arguments:
- queries: bfloat16 [4, 1024, 1024], P('section', 'seq'), may hold values from -15 to 15, as said below
- keys: bfloat16 [4, 1024, 128], P('section', 'seq'), may hold values from -6 to 6, as said below
- values: bfloat16 [4, 1024, 128], P('section', 'seq'), may hold values from -6 to 6
- cache_keys: bfloat16 [4, 8, 512, 128], P('section', 'seq'), may hold values from -6 to 6
- cache_values: bfloat16 [4, 8, 512, 128], P('section', 'seq'), may hold values from -6 to 6
- vertical: int32 [4, 8, 32], P('section', 'seq'), may hold values from 0 to 63, as said below
- vertical_count: int32 [4, 8], P('section', 'seq'), may hold values from 1 to 32, as said below
- slash: int32 [4, 8, 11], P('section', 'seq'), may hold values from 1 to 79, as said below
Outputs:
- attended: bfloat16 [4, 1024, 1024], P('section', 'seq')
The draws below stay inside these ranges and needn't reach their ends.
Inputs may be any that keep to these rules, and one draw needn't show every extreme that they name: queries within the range in both draws. keys within the range in both draws. `vertical`: for each layer and head, the 32 entries are distinct cached block indices. `vertical_count`: in every layer some head uses all 32 slots. `slash`: for each layer and head, the 11 offsets are distinct.
All inputs are finite; a program needn't handle non-finite values.
Results may differ from the reference program's by a relative error of at most 0.011.
Values may be sent and summed in bfloat16 or wider, within the bound.
A program may use at most 64 MiB of HBM per device.

```python
import math
import jax
import jax.numpy as jnp
from jax import lax

HEAD_SIZE = 128
GROUP = 8
BLK = 64
NVMAX = 32
NS = 11
CACHE = 4096
STRETCH = 1024
HQ = 8
KVH = 1
LAYERS = 4


def draw_queries(key, part):
    own_key = jax.random.fold_in(key, 1)
    base = jnp.clip(2.5 * jax.random.normal(own_key, (LAYERS, STRETCH, HQ * HEAD_SIZE)), -15.0, 15.0)
    return base.astype(jnp.bfloat16)


def draw_keys(key, part):
    own_key = jax.random.fold_in(key, 2)
    base = jnp.clip(jax.random.normal(own_key, (LAYERS, STRETCH, KVH * HEAD_SIZE)), -6.0, 6.0)
    return base.astype(jnp.bfloat16)


def draw_vertical(key, part):
    streams = jax.random.split(jax.random.fold_in(key, 3), LAYERS * HQ)
    picks = jax.vmap(lambda single: jax.random.permutation(single, CACHE // BLK)[:NVMAX])(streams)
    return picks.reshape(LAYERS, HQ, NVMAX).astype(jnp.int32)


def draw_vertical_count(key, part):
    spread = jax.random.randint(jax.random.fold_in(key, 4), (LAYERS, HQ), 0, 17)
    count = 1 + spread * spread * (NVMAX - 1) // 256
    heavy = jax.random.randint(jax.random.fold_in(key, 5), (LAYERS, 1), 0, HQ)
    count = jnp.where(jnp.arange(HQ)[None, :] == heavy, NVMAX, count)
    return count.astype(jnp.int32)


def draw_slash(key, part):
    streams = jax.random.split(jax.random.fold_in(key, 6), LAYERS * HQ)
    picks = jax.vmap(lambda single: jax.random.permutation(single, CACHE // BLK + STRETCH // BLK - 1)[:NS])(streams)
    return (picks + 1).reshape(LAYERS, HQ, NS).astype(jnp.int32)


def block_scale(key, dims, cuts, smallest, largest):
    gain, own = 1.0, jax.random.fold_in(key, 6)
    for axis_at, blocks in cuts:
        steps = jnp.exp(jax.random.uniform(jax.random.fold_in(own, axis_at), (blocks,), jnp.float32, smallest / len(cuts), largest / len(cuts)))
        gain = gain * jnp.repeat(steps, dims[axis_at] // blocks).reshape([-1 if axis == axis_at else 1 for axis in range(len(dims))])
    return gain


def noise(key, extent, scale, limit, pieces=(), held_as=jnp.bfloat16):
    result = scale * jax.random.normal(key, extent, jnp.float32)
    if pieces:
        result = result * block_scale(key, extent, pieces, -0.22, 0.18)
    return jnp.clip(result, -limit, limit).astype(held_as)


def setup_inputs(seed: int = 0) -> dict:
    streams_of = jax.random.split(jax.random.key(seed), 9)
    queries = draw_queries(jax.random.fold_in(streams_of[8], 71), 0)
    keys = draw_keys(jax.random.fold_in(streams_of[8], 71), 0)
    values = noise(streams_of[2], (LAYERS, STRETCH, KVH * HEAD_SIZE), 1.0, 6.0, ((0, 4), (1, 8)))
    cache_keys = noise(streams_of[3], (LAYERS, KVH * GROUP, CACHE // GROUP, HEAD_SIZE), 1.0, 6.0, ((0, 4), (1, 8)))
    cache_values = noise(streams_of[4], (LAYERS, KVH * GROUP, CACHE // GROUP, HEAD_SIZE), 1.0, 6.0, ((0, 4), (1, 8)))
    vertical = draw_vertical(jax.random.fold_in(streams_of[8], 71), 0)
    vertical_count = draw_vertical_count(jax.random.fold_in(streams_of[8], 71), 0)
    slash = draw_slash(jax.random.fold_in(streams_of[8], 71), 0)
    return {"queries": queries, "keys": keys, "values": values, "cache_keys": cache_keys, "cache_values": cache_values, "vertical": vertical, "vertical_count": vertical_count, "slash": slash}


big_negative = -1e+30

def head_attention(query_matrix, gathered_keys, gathered_values, verts, count, slashes):
    prefill_stretch = query_matrix.shape[0]
    ncb = CACHE // BLK
    nqb = prefill_stretch // BLK
    softmax_scale = 1.0 / math.sqrt(HEAD_SIZE)
    inner = jnp.arange(BLK, dtype=jnp.int32)
    vertical_row_index = (verts[:, None].astype(jnp.int32) * BLK + inner[None, :]).reshape(-1)
    vertical_key_rows = jnp.take(gathered_keys, vertical_row_index, axis=0)
    vertical_value_rows = jnp.take(gathered_values, vertical_row_index, axis=0)
    vlive = jnp.repeat(jnp.arange(NVMAX, dtype=jnp.int32) < count, BLK)
    vertical_block_list = jnp.dot(query_matrix, vertical_key_rows.T, preferred_element_type=jnp.float32) * softmax_scale
    offsets = jnp.concatenate([jnp.zeros((1,), jnp.int32), slashes.astype(jnp.int32)])
    blocks = ncb + jnp.arange(nqb, dtype=jnp.int32)[:, None] - offsets[None, :]
    used = jnp.arange(NVMAX, dtype=jnp.int32)[None, None, :] < count
    listed = jnp.any((blocks[:, :, None] == verts[None, None, :].astype(jnp.int32)) & used, axis=2)
    valid = (blocks >= 0) & jnp.logical_not(listed)
    safe = jnp.maximum(blocks, 0)
    width = (NS + 1) * BLK
    slash_row_index = (safe[:, :, None] * BLK + inner[None, None, :]).reshape(nqb, width)
    slash_key_rows = jnp.take(gathered_keys, slash_row_index, axis=0)
    slash_value_rows = jnp.take(gathered_values, slash_row_index, axis=0)
    query_block_count = query_matrix.reshape(nqb, BLK, HEAD_SIZE)
    slash_block_list = jnp.einsum('cra,cma->crm', query_block_count.astype(jnp.float32), slash_key_rows.astype(jnp.float32)) * softmax_scale
    column = jnp.arange(width, dtype=jnp.int32)
    causal = (column[None, :] >= BLK) | ((column % BLK)[None, :] <= inner[:, None])
    smask = jnp.repeat(valid, BLK, axis=1)[:, None, :] & causal[None, :, :]
    vtop = lax.optimization_barrier(jnp.max(jnp.where(vlive[None, :], vertical_block_list, big_negative), axis=1))
    stop = lax.optimization_barrier(jnp.max(jnp.where(smask, slash_block_list, big_negative), axis=2)).reshape(prefill_stretch)
    top = jnp.maximum(vtop, stop)
    vertical_probabilities = jnp.where(vlive[None, :], jnp.exp(vertical_block_list - top[:, None]), 0.0)
    slash_probabilities = jnp.where(smask, jnp.exp(slash_block_list - top.reshape(nqb, BLK, 1)), 0.0)
    total = lax.optimization_barrier(jnp.sum(vertical_probabilities, axis=1)) + lax.optimization_barrier(jnp.sum(slash_probabilities, axis=2)).reshape(prefill_stretch)
    output_running = jnp.dot(vertical_probabilities.astype(jnp.bfloat16), vertical_value_rows, preferred_element_type=jnp.float32)
    output_running = output_running + jnp.einsum('owu,out->owt', slash_probabilities.astype(jnp.bfloat16).astype(jnp.float32), slash_value_rows.astype(jnp.float32)).reshape(prefill_stretch, HEAD_SIZE)
    return (output_running / total[:, None]).astype(jnp.bfloat16)

def reference(queries, keys, values, cache_keys, cache_values, vertical, vertical_count, slash):
    q_in = jnp.roll(queries, 1, axis=0)
    k_in = jnp.roll(keys, 1, axis=0)
    v_in = jnp.roll(values, 1, axis=0)
    layers = queries.shape[0]
    prefill_stretch = queries.shape[1]
    heads = vertical.shape[1]

    def one(index):
        layer = index // heads
        head = index % heads
        group_id = head // GROUP
        query_matrix = lax.dynamic_slice_in_dim(lax.dynamic_index_in_dim(q_in, layer, 0, keepdims=False), head * HEAD_SIZE, HEAD_SIZE, axis=1)
        stretch_keys = lax.dynamic_slice_in_dim(lax.dynamic_index_in_dim(k_in, layer, 0, keepdims=False), group_id * HEAD_SIZE, HEAD_SIZE, axis=1)
        stretch_vals = lax.dynamic_slice_in_dim(lax.dynamic_index_in_dim(v_in, layer, 0, keepdims=False), group_id * HEAD_SIZE, HEAD_SIZE, axis=1)
        old_keys = lax.dynamic_slice_in_dim(lax.dynamic_index_in_dim(cache_keys, layer, 0, keepdims=False), group_id * GROUP, GROUP, axis=0).reshape(CACHE, HEAD_SIZE)
        old_vals = lax.dynamic_slice_in_dim(lax.dynamic_index_in_dim(cache_values, layer, 0, keepdims=False), group_id * GROUP, GROUP, axis=0).reshape(CACHE, HEAD_SIZE)
        gathered_keys = jnp.concatenate([old_keys, stretch_keys], axis=0)
        gathered_values = jnp.concatenate([old_vals, stretch_vals], axis=0)
        verts = vertical[layer, head]
        count = vertical_count[layer, head]
        slashes = slash[layer, head]
        return head_attention(query_matrix, gathered_keys, gathered_values, verts, count, slashes)
    outcome = lax.map(one, jnp.arange(layers * heads, dtype=jnp.int32))
    outcome = outcome.reshape(layers, heads, prefill_stretch, HEAD_SIZE).transpose(0, 2, 1, 3)
    return outcome.reshape(layers, prefill_stretch, heads * HEAD_SIZE)
```

```python
import functools
import math

import jax
import jax.numpy as jnp
from jax import lax
from jax.experimental import pallas as pl
from jax.experimental.pallas import tpu as pltpu
from jax.sharding import PartitionSpec as P

HEAD = 128
GROUP = 8
BLK = 64
NVMAX = 32
NS = 11
LANES = 128
MASKED = -1e30
MESH = pl.DeviceIdType.MESH
UP, DOWN, ACROSS = 0, 1, 2
CK, CV, SK, SV = 0, 1, 2, 3


def kernel(
    layers,
    n,
    q_hbm,
    k_hbm,
    v_hbm,
    ck_hbm,
    cv_hbm,
    vert_ref,
    count_ref,
    slash_ref,
    out_ref,
    ckbuf,
    cvbuf,
    skbuf,
    svbuf,
    qbuf,
    tabs,
    tabr,
    qaug,
    acc,
    top,
    local_sem,
    shift_send,
    q_recv,
    send_sem,
    recv_sem,
    tab_send,
    tab_recv,
):
    tok = qbuf.shape[0]
    part = ckbuf.shape[1]
    kvh = skbuf.shape[2] // HEAD
    per = tok // BLK
    ncb = GROUP * part // BLK
    nqb = n * per
    rows_of_group = GROUP * tok
    tile = min(2 * tok, rows_of_group)
    outer = n // 2
    sec = lax.axis_index("section")
    me = lax.axis_index("seq")
    o, i = me // 2, me % 2
    after, before = lax.rem(sec + 1, layers), lax.rem(sec + layers - 1, layers)
    scale = math.log2(math.e) / math.sqrt(HEAD)

    barrier = pltpu.get_barrier_semaphore()
    for d in range(1, n):
        pl.semaphore_signal(
            barrier, inc=1, device_id={"seq": lax.rem(me + d, n)}, device_id_type=MESH
        )
    for other in (after, before):
        pl.semaphore_signal(barrier, inc=1, device_id={"section": other}, device_id_type=MESH)
    pl.semaphore_wait(barrier, n + 1)

    bufs = (ckbuf, cvbuf, skbuf, svbuf)
    target = (me + 2, me - 2, me + 1 - 2 * i)

    def relay(which, slot, way, src=None):
        dst = bufs[which].at[slot]
        return pltpu.make_async_remote_copy(
            src_ref=dst if src is None else src,
            dst_ref=dst,
            send_sem=send_sem.at[way, which, slot],
            recv_sem=recv_sem.at[which, slot],
            device_id={"seq": target[way]},
            device_id_type=MESH,
        )

    def shift(src, dst, index, recv):
        return pltpu.make_async_remote_copy(
            src_ref=src,
            dst_ref=dst,
            send_sem=shift_send.at[index],
            recv_sem=recv,
            device_id={"section": after},
            device_id_type=MESH,
        )

    shifts = (
        shift(k_hbm, skbuf.at[me], 0, recv_sem.at[SK, me]),
        shift(v_hbm, svbuf.at[me], 1, recv_sem.at[SV, me]),
        shift(q_hbm, qbuf, 2, q_recv),
    )
    for copy in shifts:
        copy.start()
    own = ((CK, ck_hbm), (CV, cv_hbm))
    for which, src in own:
        relay(which, me, ACROSS, src).start()

        @pl.when(o < outer - 1)
        def _():
            relay(which, me, UP, src).start()

        @pl.when(o > 0)
        def _():
            relay(which, me, DOWN, src).start()

    locals_ = [
        pltpu.make_async_copy(src, bufs[which].at[me], local_sem.at[which]) for which, src in own
    ]
    for copy in locals_:
        copy.start()

    lane = lax.broadcasted_iota(jnp.int32, (1, LANES), 1)
    count = count_ref[0, 0]
    hit = lane < 0
    for slot in range(NVMAX):
        hit = hit | (lane == jnp.where(slot < count, vert_ref[0, slot], -1))
    listed = jnp.where(hit, 1, 0)
    offsets = [slash_ref[0, j] for j in range(NS)]

    def fill(b, carry):
        diagonal = ncb + b
        found = (listed > 0) | (lane == diagonal)
        for off in offsets:
            found = found | (lane == diagonal - off)
        tabs[b] = jnp.where(found, 0.0, MASKED)
        return carry

    lax.fori_loop(0, nqb, fill, 0)

    def table(d):
        to = lax.rem(me + d, n)
        return pltpu.make_async_remote_copy(
            src_ref=tabs.at[pl.ds(to * per, per)],
            dst_ref=tabr.at[me],
            send_sem=tab_send.at[d],
            recv_sem=tab_recv.at[me],
            device_id={"seq": to},
            device_id_type=MESH,
        )

    for d in range(1, n):
        table(d).start()
    tabr[me] = tabs[pl.ds(me * per, per)]

    for which in (SK, SV):
        relay(which, me, UP).wait_recv()

        @pl.when(o < outer - 1)
        def _():
            relay(which, me, UP).start()

        @pl.when(i == 0)
        def _():
            relay(which, me, ACROSS).start()

    shifts[2].wait_recv()
    for d in range(1, n):
        src = lax.rem(me + d, n)
        pltpu.make_async_remote_copy(
            src_ref=tabs.at[pl.ds(0, per)],
            dst_ref=tabr.at[src],
            send_sem=tab_send.at[d],
            recv_sem=tab_recv.at[src],
            device_id={"seq": src},
            device_id_type=MESH,
        ).wait_recv()
    for h in range(n):
        qaug[h * tok : (h + 1) * tok, :HEAD] = qbuf[:, h * HEAD : (h + 1) * HEAD]
        for j in range(per):
            qaug[h * tok + j * BLK : h * tok + (j + 1) * BLK, HEAD:] = jnp.broadcast_to(
                tabr[h, j].astype(jnp.bfloat16), (BLK, LANES)
            )

    def attend(keys, values, first_block, base, diagonal=False):
        width = keys.shape[0]
        block = lax.broadcasted_iota(jnp.int32, (width, LANES), 0) // BLK + first_block
        mark = lax.broadcasted_iota(jnp.int32, (width, LANES), 1) == block
        keys = jnp.concatenate([keys, jnp.where(mark, 1.0, 0.0).astype(jnp.bfloat16)], axis=1)
        values = jnp.concatenate([values, jnp.ones((width, LANES), jnp.bfloat16)], axis=1)
        span = width // LANES

        def body(step, carry):
            rows = pl.ds(pl.multiple_of(base + step * tile, tile), tile)
            scores = lax.dot_general(
                qaug[rows, :], keys, (((1,), (1,)), ((), ())), preferred_element_type=jnp.float32
            )
            if diagonal:
                token = lax.rem(lax.broadcasted_iota(jnp.int32, (tile, width), 0), tok)
                key = lax.broadcasted_iota(jnp.int32, (tile, width), 1)
                scores = jnp.where(key <= token, scores, MASKED)
            high = jnp.broadcast_to(jnp.max(scores, axis=1, keepdims=True), (tile, LANES))
            if not diagonal:
                old = top[rows, :]
                high = jnp.maximum(old, high)
            top[rows, :] = high
            wide = jnp.concatenate([high] * span, axis=1)
            weights = jnp.exp2((scores - wide) * scale).astype(jnp.bfloat16)
            fresh = jnp.dot(weights, values, preferred_element_type=jnp.float32)
            if diagonal:
                acc[rows, :] = fresh
            else:
                factor = jnp.exp2((old - high) * scale)
                acc[rows, :] = acc[rows, :] * jnp.concatenate([factor] * 2, axis=1) + fresh
            return carry

        lax.fori_loop(0, rows_of_group // tile, body, 0)

    def attend_cache(slot):
        attend(
            ckbuf[slot],
            cvbuf[slot],
            lax.rem(slot, GROUP) * (part // BLK),
            slot // GROUP * rows_of_group,
        )

    def attend_stretch(slot, slots, diagonal=False):
        for g in range(kvh):
            keys = skbuf[pl.ds(slot, slots), :, g * HEAD : (g + 1) * HEAD]
            values = svbuf[pl.ds(slot, slots), :, g * HEAD : (g + 1) * HEAD]
            attend(
                keys.reshape(slots * tok, HEAD),
                values.reshape(slots * tok, HEAD),
                ncb + slot * per,
                g * rows_of_group,
                diagonal,
            )

    attend_stretch(me, 1, diagonal=True)
    for copy in locals_:
        copy.wait()
    attend_cache(me)

    def across(k):
        low, high = me - 2 * k + 1 - 2 * i, me + 2 * k + 1 - 2 * i

        @pl.when(o - k >= 0)
        def _():
            for which in (CK, CV, SK, SV):
                relay(which, low, ACROSS).wait_recv()
            attend_cache(low)
            attend_stretch((o - k) * 2, 2)

        @pl.when(o + k < outer)
        def _():
            for which in (CK, CV):
                relay(which, high, ACROSS).wait_recv()
            attend_cache(high)

    def step(k, carry):
        low, high = me - 2 * k, me + 2 * k

        @pl.when(o - k >= 0)
        def _():
            for which in (CK, CV, SK, SV):
                relay(which, low, UP).wait_recv()

                @pl.when(o < outer - 1)
                def _():
                    relay(which, low, UP).start()

                relay(which, low, ACROSS).start()

        @pl.when(o + k < outer)
        def _():
            for which in (CK, CV):
                relay(which, high, DOWN).wait_recv()

                @pl.when(o > 0)
                def _():
                    relay(which, high, DOWN).start()

                relay(which, high, ACROSS).start()

        @pl.when(k > 1)
        def _():
            across(k - 1)

        @pl.when(k == 1)
        def _():
            partner = me + 1 - 2 * i
            for which in (CK, CV):
                relay(which, partner, ACROSS).wait_recv()
            attend_cache(partner)

            @pl.when(i == 1)
            def _():
                for which in (SK, SV):
                    relay(which, partner, ACROSS).wait_recv()
                attend_stretch(partner, 1)

        @pl.when(o - k >= 0)
        def _():
            attend_cache(low)

        @pl.when(o + k < outer)
        def _():
            attend_cache(high)

        return carry

    lax.fori_loop(1, outer, step, 0)
    across(outer - 1)

    for h in range(n):
        rows = slice(h * tok, (h + 1) * tok)
        out_ref[:, h * HEAD : (h + 1) * HEAD] = (acc[rows, :HEAD] / acc[rows, HEAD:]).astype(
            out_ref.dtype
        )

    for copy in shifts:
        copy.wait_send()
    for d in range(1, n):
        table(d).wait_send()
    for which, src in own:
        relay(which, me, ACROSS, src).wait_send()

        @pl.when(o < outer - 1)
        def _():
            relay(which, me, UP, src).wait_send()

        @pl.when(o > 0)
        def _():
            relay(which, me, DOWN, src).wait_send()

    for which in (SK, SV):

        @pl.when(o < outer - 1)
        def _():
            relay(which, me, UP).wait_send()

        @pl.when(i == 0)
        def _():
            relay(which, me, ACROSS).wait_send()

    def drain(k, carry):
        low, high = me - 2 * k, me + 2 * k

        @pl.when(o - k >= 0)
        def _():
            for which in (CK, CV, SK, SV):

                @pl.when(o < outer - 1)
                def _():
                    relay(which, low, UP).wait_send()

                relay(which, low, ACROSS).wait_send()

        @pl.when(o + k < outer)
        def _():
            for which in (CK, CV):

                @pl.when(o > 0)
                def _():
                    relay(which, high, DOWN).wait_send()

                relay(which, high, ACROSS).wait_send()

        return carry

    lax.fori_loop(1, outer, drain, 0)


def solution(mesh):
    layers, n = mesh.shape["section"], mesh.shape["seq"]

    def per_device(queries, keys, values, cache_keys, cache_values, vertical, count, slash):
        tok, wide = queries.shape[1:]
        kv_wide = keys.shape[2]
        part = cache_keys.shape[2]
        per = tok // BLK
        dtype = queries.dtype
        rows = n * tok
        anywhere = pl.BlockSpec(memory_space=pl.ANY)
        scalars = pl.BlockSpec(memory_space=pltpu.SMEM)
        keys_all = GROUP * part + n * tok
        result = pl.pallas_call(
            functools.partial(kernel, layers, n),
            out_shape=jax.ShapeDtypeStruct((tok, wide), dtype),
            in_specs=[anywhere] * 5 + [scalars] * 3,
            out_specs=pl.BlockSpec(memory_space=pltpu.VMEM),
            scratch_shapes=[
                pltpu.VMEM((n, part, HEAD), dtype),
                pltpu.VMEM((n, part, HEAD), dtype),
                pltpu.VMEM((n, tok, kv_wide), dtype),
                pltpu.VMEM((n, tok, kv_wide), dtype),
                pltpu.VMEM((tok, wide), dtype),
                pltpu.VMEM((n * per, 1, LANES), jnp.float32),
                pltpu.VMEM((n, per, 1, LANES), jnp.float32),
                pltpu.VMEM((rows, 2 * HEAD), dtype),
                pltpu.VMEM((rows, 2 * HEAD), jnp.float32),
                pltpu.VMEM((rows, LANES), jnp.float32),
                pltpu.SemaphoreType.DMA((2,)),
                pltpu.SemaphoreType.DMA((3,)),
                pltpu.SemaphoreType.DMA,
                pltpu.SemaphoreType.DMA((3, 4, n)),
                pltpu.SemaphoreType.DMA((4, n)),
                pltpu.SemaphoreType.DMA((n,)),
                pltpu.SemaphoreType.DMA((n,)),
            ],
            compiler_params=pltpu.CompilerParams(
                collective_id=0, has_side_effects=True, vmem_limit_bytes=50 * 2**20
            ),
            cost_estimate=pl.CostEstimate(
                flops=4 * rows * keys_all * HEAD,
                bytes_accessed=2 * rows * HEAD * 4,
                transcendentals=rows * keys_all,
            ),
        )(
            queries[0],
            keys[0],
            values[0],
            cache_keys[0, 0],
            cache_values[0, 0],
            vertical[0],
            count,
            slash[0],
        )
        return result[None]

    return jax.shard_map(
        per_device,
        mesh=mesh,
        in_specs=(
            P("section", "seq", None),
            P("section", "seq", None),
            P("section", "seq", None),
            P("section", "seq", None, None),
            P("section", "seq", None, None),
            P("section", "seq", None),
            P("section", "seq"),
            P("section", "seq", None),
        ),
        out_specs=P("section", "seq", None),
        check_vma=False,
    )
```

```python
import functools
import math

import jax
import jax.numpy as jnp
from jax import lax
from jax.experimental import pallas as pl
from jax.experimental.pallas import tpu as pltpu
from jax.sharding import PartitionSpec as P

HEAD = 128
GROUP = 8
BLK = 64
NVMAX = 32
NS = 11
LANES = 128
MASKED = -1e30
MESH = pl.DeviceIdType.MESH
UP, DOWN, ACROSS = 0, 1, 2
CK, CV, SK, SV = 0, 1, 2, 3


def kernel(
    layers,
    n,
    q_hbm,
    k_hbm,
    v_hbm,
    ck_hbm,
    cv_hbm,
    vert_ref,
    count_ref,
    slash_ref,
    out_ref,
    ckbuf,
    cvbuf,
    skbuf,
    svbuf,
    qbuf,
    tabs,
    tabr,
    qaug,
    acc,
    top,
    local_sem,
    shift_send,
    q_recv,
    send_sem,
    recv_sem,
    tab_send,
    tab_recv,
):
    tok = qbuf.shape[0]
    part = ckbuf.shape[1]
    kvh = skbuf.shape[2] // HEAD
    per = tok // BLK
    ncb = GROUP * part // BLK
    nqb = n * per
    rows_of_group = GROUP * tok
    tile = min(2 * tok, rows_of_group)
    outer = n // 2
    sec = lax.axis_index("section")
    me = lax.axis_index("seq")
    o, i = me // 2, me % 2
    after, before = lax.rem(sec + 1, layers), lax.rem(sec + layers - 1, layers)
    scale = math.log2(math.e) / math.sqrt(HEAD)

    barrier = pltpu.get_barrier_semaphore()
    for d in range(1, n):
        pl.semaphore_signal(
            barrier, inc=1, device_id={"seq": lax.rem(me + d, n)}, device_id_type=MESH
        )
    for other in (after, before):
        pl.semaphore_signal(barrier, inc=1, device_id={"section": other}, device_id_type=MESH)
    pl.semaphore_wait(barrier, n + 1)

    bufs = (ckbuf, cvbuf, skbuf, svbuf)
    target = (me + 2, me - 2, me + 1 - 2 * i)

    def relay(which, slot, way, src=None):
        dst = bufs[which].at[slot]
        return pltpu.make_async_remote_copy(
            src_ref=dst if src is None else src,
            dst_ref=dst,
            send_sem=send_sem.at[way, which, slot],
            recv_sem=recv_sem.at[which, slot],
            device_id={"seq": target[way]},
            device_id_type=MESH,
        )

    def shift(src, dst, index, recv):
        return pltpu.make_async_remote_copy(
            src_ref=src,
            dst_ref=dst,
            send_sem=shift_send.at[index],
            recv_sem=recv,
            device_id={"section": after},
            device_id_type=MESH,
        )

    shifts = (
        shift(k_hbm, skbuf.at[me], 0, recv_sem.at[SK, me]),
        shift(v_hbm, svbuf.at[me], 1, recv_sem.at[SV, me]),
        shift(q_hbm, qbuf, 2, q_recv),
    )
    for copy in shifts:
        copy.start()
    own = ((CK, ck_hbm), (CV, cv_hbm))
    for which, src in own:
        relay(which, me, ACROSS, src).start()

        @pl.when(o < outer - 1)
        def _():
            relay(which, me, UP, src).start()

        @pl.when(o > 0)
        def _():
            relay(which, me, DOWN, src).start()

    locals_ = [
        pltpu.make_async_copy(src, bufs[which].at[me], local_sem.at[which]) for which, src in own
    ]
    for copy in locals_:
        copy.start()

    lane = lax.broadcasted_iota(jnp.int32, (1, LANES), 1)
    count = count_ref[0, 0]
    hit = lane < 0
    for slot in range(NVMAX):
        hit = hit | (lane == jnp.where(slot < count, vert_ref[0, slot], -1))
    listed = jnp.where(hit, 1, 0)
    offsets = [slash_ref[0, j] for j in range(NS)]

    def fill(b, carry):
        diagonal = ncb + b
        found = (listed > 0) | (lane == diagonal)
        for off in offsets:
            found = found | (lane == diagonal - off)
        tabs[b] = jnp.where(found, 0.0, MASKED)
        return carry

    lax.fori_loop(0, nqb, fill, 0)

    def table(d):
        to = lax.rem(me + d, n)
        return pltpu.make_async_remote_copy(
            src_ref=tabs.at[pl.ds(to * per, per)],
            dst_ref=tabr.at[me],
            send_sem=tab_send.at[d],
            recv_sem=tab_recv.at[me],
            device_id={"seq": to},
            device_id_type=MESH,
        )

    for d in range(1, n):
        table(d).start()
    tabr[me] = tabs[pl.ds(me * per, per)]

    for which in (SK, SV):
        relay(which, me, UP).wait_recv()

        @pl.when(o < outer - 1)
        def _():
            relay(which, me, UP).start()

        @pl.when(i == 0)
        def _():
            relay(which, me, ACROSS).start()

    shifts[2].wait_recv()
    for d in range(1, n):
        src = lax.rem(me + d, n)
        pltpu.make_async_remote_copy(
            src_ref=tabs.at[pl.ds(0, per)],
            dst_ref=tabr.at[src],
            send_sem=tab_send.at[d],
            recv_sem=tab_recv.at[src],
            device_id={"seq": src},
            device_id_type=MESH,
        ).wait_recv()
    for h in range(n):
        qaug[h * tok : (h + 1) * tok, :HEAD] = qbuf[:, h * HEAD : (h + 1) * HEAD]
        for j in range(per):
            qaug[h * tok + j * BLK : h * tok + (j + 1) * BLK, HEAD:] = jnp.broadcast_to(
                tabr[h, j].astype(jnp.bfloat16), (BLK, LANES)
            )

    def attend(keys, values, first_block, base, diagonal=False):
        width = keys.shape[0]
        block = lax.broadcasted_iota(jnp.int32, (width, LANES), 0) // BLK + first_block
        mark = lax.broadcasted_iota(jnp.int32, (width, LANES), 1) == block
        keys = jnp.concatenate([keys, jnp.where(mark, 1.0, 0.0).astype(jnp.bfloat16)], axis=1)
        values = jnp.concatenate([values, jnp.ones((width, LANES), jnp.bfloat16)], axis=1)
        span = width // LANES

        def scores_of(rows):
            scores = lax.dot_general(
                qaug[rows, :], keys, (((1,), (1,)), ((), ())), preferred_element_type=jnp.float32
            )
            if diagonal:
                token = lax.rem(lax.broadcasted_iota(jnp.int32, (tile, width), 0), tok)
                key = lax.broadcasted_iota(jnp.int32, (tile, width), 1)
                scores = jnp.where(key <= token, scores, MASKED)
            return scores

        def update(rows, scores):
            high = jnp.broadcast_to(jnp.max(scores, axis=1, keepdims=True), (tile, LANES))
            if not diagonal:
                old = top[rows, :]
                high = jnp.maximum(old, high)
            top[rows, :] = high
            wide = jnp.concatenate([high] * span, axis=1)
            weights = jnp.exp2((scores - wide) * scale).astype(jnp.bfloat16)
            fresh = jnp.dot(weights, values, preferred_element_type=jnp.float32)
            if diagonal:
                acc[rows, :] = fresh
            else:
                factor = jnp.exp2((old - high) * scale)
                acc[rows, :] = acc[rows, :] * jnp.concatenate([factor] * 2, axis=1) + fresh

        spans = [
            pl.ds(base + t * tile if kvh == 1 else pl.multiple_of(base + t * tile, tile), tile)
            for t in range(rows_of_group // tile)
        ]
        ahead = scores_of(spans[0])
        for t, rows in enumerate(spans):
            scores = ahead
            if t + 1 < len(spans):
                ahead = scores_of(spans[t + 1])
            update(rows, scores)

    def attend_cache(slot):
        attend(
            ckbuf[slot],
            cvbuf[slot],
            lax.rem(slot, GROUP) * (part // BLK),
            0 if kvh == 1 else slot // GROUP * rows_of_group,
        )

    def attend_stretch(slot, slots, diagonal=False):
        for g in range(kvh):
            keys = skbuf[pl.ds(slot, slots), :, g * HEAD : (g + 1) * HEAD]
            values = svbuf[pl.ds(slot, slots), :, g * HEAD : (g + 1) * HEAD]
            attend(
                keys.reshape(slots * tok, HEAD),
                values.reshape(slots * tok, HEAD),
                ncb + slot * per,
                g * rows_of_group,
                diagonal,
            )

    attend_stretch(me, 1, diagonal=True)
    for copy in locals_:
        copy.wait()
    attend_cache(me)

    def across(k):
        low, high = me - 2 * k + 1 - 2 * i, me + 2 * k + 1 - 2 * i

        @pl.when(o - k >= 0)
        def _():
            for which in (CK, CV, SK, SV):
                relay(which, low, ACROSS).wait_recv()
            attend_cache(low)
            attend_stretch((o - k) * 2, 2)

        @pl.when(o + k < outer)
        def _():
            for which in (CK, CV):
                relay(which, high, ACROSS).wait_recv()
            attend_cache(high)

    def step(k, carry):
        low, high = me - 2 * k, me + 2 * k

        def pass_up(*arrays):
            @pl.when(o - k >= 0)
            def _():
                for which in arrays:
                    relay(which, low, UP).wait_recv()

                    @pl.when(o < outer - 1)
                    def _():
                        relay(which, low, UP).start()

                    relay(which, low, ACROSS).start()

        def pass_down(*arrays):
            @pl.when(o + k < outer)
            def _():
                for which in arrays:
                    relay(which, high, DOWN).wait_recv()

                    @pl.when(o > 0)
                    def _():
                        relay(which, high, DOWN).start()

                    relay(which, high, ACROSS).start()

        pass_up(CK)
        pass_down(CK)
        pass_up(CV)
        pass_down(CV)
        pass_up(SK, SV)

        @pl.when(k > 1)
        def _():
            across(k - 1)

        @pl.when(k == 1)
        def _():
            partner = me + 1 - 2 * i
            for which in (CK, CV):
                relay(which, partner, ACROSS).wait_recv()
            attend_cache(partner)

            @pl.when(i == 1)
            def _():
                for which in (SK, SV):
                    relay(which, partner, ACROSS).wait_recv()
                attend_stretch(partner, 1)

        @pl.when(o - k >= 0)
        def _():
            attend_cache(low)

        @pl.when(o + k < outer)
        def _():
            attend_cache(high)

        return carry

    lax.fori_loop(1, outer, step, 0)
    across(outer - 1)

    for h in range(n):
        rows = slice(h * tok, (h + 1) * tok)
        out_ref[:, h * HEAD : (h + 1) * HEAD] = (acc[rows, :HEAD] / acc[rows, HEAD:]).astype(
            out_ref.dtype
        )

    for copy in shifts:
        copy.wait_send()
    for d in range(1, n):
        table(d).wait_send()
    for which, src in own:
        relay(which, me, ACROSS, src).wait_send()

        @pl.when(o < outer - 1)
        def _():
            relay(which, me, UP, src).wait_send()

        @pl.when(o > 0)
        def _():
            relay(which, me, DOWN, src).wait_send()

    for which in (SK, SV):

        @pl.when(o < outer - 1)
        def _():
            relay(which, me, UP).wait_send()

        @pl.when(i == 0)
        def _():
            relay(which, me, ACROSS).wait_send()

    def drain(k, carry):
        low, high = me - 2 * k, me + 2 * k

        @pl.when(o - k >= 0)
        def _():
            for which in (CK, CV, SK, SV):

                @pl.when(o < outer - 1)
                def _():
                    relay(which, low, UP).wait_send()

                relay(which, low, ACROSS).wait_send()

        @pl.when(o + k < outer)
        def _():
            for which in (CK, CV):

                @pl.when(o > 0)
                def _():
                    relay(which, high, DOWN).wait_send()

                relay(which, high, ACROSS).wait_send()

        return carry

    lax.fori_loop(1, outer, drain, 0)


def solution(mesh):
    layers, n = mesh.shape["section"], mesh.shape["seq"]

    def per_device(queries, keys, values, cache_keys, cache_values, vertical, count, slash):
        tok, wide = queries.shape[1:]
        kv_wide = keys.shape[2]
        part = cache_keys.shape[2]
        per = tok // BLK
        dtype = queries.dtype
        rows = n * tok
        anywhere = pl.BlockSpec(memory_space=pltpu.HBM)
        scalars = pl.BlockSpec(memory_space=pltpu.SMEM)
        keys_all = GROUP * part + n * tok
        result = pl.pallas_call(
            functools.partial(kernel, layers, n),
            out_shape=jax.ShapeDtypeStruct((tok, wide), dtype),
            in_specs=[anywhere] * 5 + [scalars] * 3,
            out_specs=pl.BlockSpec(memory_space=pltpu.VMEM),
            scratch_shapes=[
                pltpu.VMEM((n, part, HEAD), dtype),
                pltpu.VMEM((n, part, HEAD), dtype),
                pltpu.VMEM((n, tok, kv_wide), dtype),
                pltpu.VMEM((n, tok, kv_wide), dtype),
                pltpu.VMEM((tok, wide), dtype),
                pltpu.VMEM((n * per, 1, LANES), jnp.float32),
                pltpu.VMEM((n, per, 1, LANES), jnp.float32),
                pltpu.VMEM((rows, 2 * HEAD), dtype),
                pltpu.VMEM((rows, 2 * HEAD), jnp.float32),
                pltpu.VMEM((rows, LANES), jnp.float32),
                pltpu.SemaphoreType.DMA((2,)),
                pltpu.SemaphoreType.DMA((3,)),
                pltpu.SemaphoreType.DMA,
                pltpu.SemaphoreType.DMA((3, 4, n)),
                pltpu.SemaphoreType.DMA((4, n)),
                pltpu.SemaphoreType.DMA((n,)),
                pltpu.SemaphoreType.DMA((n,)),
            ],
            compiler_params=pltpu.CompilerParams(
                collective_id=0, has_side_effects=True, vmem_limit_bytes=63 * 2**20
            ),
            cost_estimate=pl.CostEstimate(
                flops=4 * rows * keys_all * HEAD,
                bytes_accessed=2 * rows * HEAD * 4,
                transcendentals=rows * keys_all,
            ),
        )(
            queries[0],
            keys[0],
            values[0],
            cache_keys[0, 0],
            cache_values[0, 0],
            vertical[0],
            count,
            slash[0],
        )
        return result[None]

    return jax.shard_map(
        per_device,
        mesh=mesh,
        in_specs=(
            P("section", "seq", None),
            P("section", "seq", None),
            P("section", "seq", None),
            P("section", "seq", None, None),
            P("section", "seq", None, None),
            P("section", "seq", None),
            P("section", "seq"),
            P("section", "seq", None),
        ),
        out_specs=P("section", "seq", None),
        check_vma=False,
    )
```

```python
import functools
import math

import jax
import jax.numpy as jnp
from jax import lax
from jax.experimental import pallas as pl
from jax.experimental.pallas import tpu as pltpu
from jax.sharding import PartitionSpec as P

HEAD = 128
GROUP = 8
BLK = 64
NVMAX = 32
NS = 11
LANES = 128
MASKED = -1e30
MESH = pl.DeviceIdType.MESH
UP, DOWN, ACROSS = 0, 1, 2
CK, CV, SK, SV = 0, 1, 2, 3


def kernel(
    layers,
    n,
    q_hbm,
    k_hbm,
    v_hbm,
    ck_hbm,
    cv_hbm,
    vert_ref,
    count_ref,
    slash_ref,
    out_ref,
    ckbuf,
    cvbuf,
    skbuf,
    svbuf,
    qbuf,
    tabs,
    tabr,
    qaug,
    acc,
    top,
    local_sem,
    shift_send,
    q_recv,
    send_sem,
    recv_sem,
    tab_send,
    tab_recv,
):
    tok = qbuf.shape[0]
    part = ckbuf.shape[1]
    kvh = skbuf.shape[2] // HEAD
    per = tok // BLK
    ncb = GROUP * part // BLK
    nqb = n * per
    rows_of_group = GROUP * tok
    tile = min(4 * tok, rows_of_group)
    outer = n // 2
    sec = lax.axis_index("section")
    me = lax.axis_index("seq")
    o, i = me // 2, me % 2
    after, before = lax.rem(sec + 1, layers), lax.rem(sec + layers - 1, layers)
    scale = math.log2(math.e) / math.sqrt(HEAD)

    barrier = pltpu.get_barrier_semaphore()
    for d in range(1, n):
        pl.semaphore_signal(
            barrier, inc=1, device_id={"seq": lax.rem(me + d, n)}, device_id_type=MESH
        )
    for other in (after, before):
        pl.semaphore_signal(barrier, inc=1, device_id={"section": other}, device_id_type=MESH)
    pl.semaphore_wait(barrier, n + 1)

    bufs = (ckbuf, cvbuf, skbuf, svbuf)
    target = (me + 2, me - 2, me + 1 - 2 * i)

    def relay(which, slot, way, src=None):
        dst = bufs[which].at[slot]
        return pltpu.make_async_remote_copy(
            src_ref=dst if src is None else src,
            dst_ref=dst,
            send_sem=send_sem.at[way, which, slot],
            recv_sem=recv_sem.at[which, slot],
            device_id={"seq": target[way]},
            device_id_type=MESH,
        )

    def shift(src, dst, index, recv):
        return pltpu.make_async_remote_copy(
            src_ref=src,
            dst_ref=dst,
            send_sem=shift_send.at[index],
            recv_sem=recv,
            device_id={"section": after},
            device_id_type=MESH,
        )

    shifts = (
        shift(k_hbm, skbuf.at[me], 0, recv_sem.at[SK, me]),
        shift(v_hbm, svbuf.at[me], 1, recv_sem.at[SV, me]),
        shift(q_hbm, qbuf, 2, q_recv),
    )
    for copy in shifts:
        copy.start()
    own = ((CK, ck_hbm), (CV, cv_hbm))
    for which, src in own:
        relay(which, me, ACROSS, src).start()

        @pl.when(o < outer - 1)
        def _():
            relay(which, me, UP, src).start()

        @pl.when(o > 0)
        def _():
            relay(which, me, DOWN, src).start()

    locals_ = [
        pltpu.make_async_copy(src, bufs[which].at[me], local_sem.at[which]) for which, src in own
    ]
    for copy in locals_:
        copy.start()

    lane = lax.broadcasted_iota(jnp.int32, (1, LANES), 1)
    count = count_ref[0, 0]
    hit = lane < 0
    for slot in range(NVMAX):
        hit = hit | (lane == jnp.where(slot < count, vert_ref[0, slot], -1))
    listed = jnp.where(hit, 1, 0)
    offsets = [slash_ref[0, j] for j in range(NS)]

    def fill(b, carry):
        diagonal = ncb + b
        found = (listed > 0) | (lane == diagonal)
        for off in offsets:
            found = found | (lane == diagonal - off)
        tabs[b] = jnp.where(found, 0.0, MASKED)
        return carry

    lax.fori_loop(0, nqb, fill, 0)

    def table(d):
        to = lax.rem(me + d, n)
        return pltpu.make_async_remote_copy(
            src_ref=tabs.at[pl.ds(to * per, per)],
            dst_ref=tabr.at[me],
            send_sem=tab_send.at[d],
            recv_sem=tab_recv.at[me],
            device_id={"seq": to},
            device_id_type=MESH,
        )

    for d in range(1, n):
        table(d).start()
    tabr[me] = tabs[pl.ds(me * per, per)]

    for which in (SK, SV):
        relay(which, me, UP).wait_recv()

        @pl.when(o < outer - 1)
        def _():
            relay(which, me, UP).start()

        @pl.when(i == 0)
        def _():
            relay(which, me, ACROSS).start()

    shifts[2].wait_recv()
    for d in range(1, n):
        src = lax.rem(me + d, n)
        pltpu.make_async_remote_copy(
            src_ref=tabs.at[pl.ds(0, per)],
            dst_ref=tabr.at[src],
            send_sem=tab_send.at[d],
            recv_sem=tab_recv.at[src],
            device_id={"seq": src},
            device_id_type=MESH,
        ).wait_recv()
    for h in range(n):
        qaug[h * tok : (h + 1) * tok, :HEAD] = qbuf[:, h * HEAD : (h + 1) * HEAD]
        for j in range(per):
            qaug[h * tok + j * BLK : h * tok + (j + 1) * BLK, HEAD:] = jnp.broadcast_to(
                tabr[h, j].astype(jnp.bfloat16), (BLK, LANES)
            )

    def attend(keys, values, first_block, base, diagonal=False):
        width = keys.shape[0]
        block = lax.broadcasted_iota(jnp.int32, (width, LANES), 0) // BLK + first_block
        mark = lax.broadcasted_iota(jnp.int32, (width, LANES), 1) == block
        keys = jnp.concatenate([keys, jnp.where(mark, 1.0, 0.0).astype(jnp.bfloat16)], axis=1)
        values = jnp.concatenate([values, jnp.ones((width, LANES), jnp.bfloat16)], axis=1)
        span = width // LANES

        def scores_of(rows):
            scores = lax.dot_general(
                qaug[rows, :], keys, (((1,), (1,)), ((), ())), preferred_element_type=jnp.float32
            )
            if diagonal:
                token = lax.rem(lax.broadcasted_iota(jnp.int32, (tile, width), 0), tok)
                key = lax.broadcasted_iota(jnp.int32, (tile, width), 1)
                scores = jnp.where(key <= token, scores, MASKED)
            return scores

        def update(rows, scores):
            high = jnp.broadcast_to(jnp.max(scores, axis=1, keepdims=True), (tile, LANES))
            if not diagonal:
                old = top[rows, :]
                high = jnp.maximum(old, high)
            top[rows, :] = high
            wide = jnp.concatenate([high] * span, axis=1)
            weights = jnp.exp2((scores - wide) * scale).astype(jnp.bfloat16)
            fresh = jnp.dot(weights, values, preferred_element_type=jnp.float32)
            if diagonal:
                acc[rows, :] = fresh
            else:
                factor = jnp.exp2((old - high) * scale)
                acc[rows, :] = acc[rows, :] * jnp.concatenate([factor] * 2, axis=1) + fresh

        spans = [
            pl.ds(base + t * tile if kvh == 1 else pl.multiple_of(base + t * tile, tile), tile)
            for t in range(rows_of_group // tile)
        ]
        ahead = scores_of(spans[0])
        for t, rows in enumerate(spans):
            scores = ahead
            if t + 1 < len(spans):
                ahead = scores_of(spans[t + 1])
            update(rows, scores)

    def attend_cache(slot):
        attend(
            ckbuf[slot],
            cvbuf[slot],
            lax.rem(slot, GROUP) * (part // BLK),
            0 if kvh == 1 else slot // GROUP * rows_of_group,
        )

    def attend_stretch(slot, slots, diagonal=False):
        for g in range(kvh):
            keys = skbuf[pl.ds(slot, slots), :, g * HEAD : (g + 1) * HEAD]
            values = svbuf[pl.ds(slot, slots), :, g * HEAD : (g + 1) * HEAD]
            attend(
                keys.reshape(slots * tok, HEAD),
                values.reshape(slots * tok, HEAD),
                ncb + slot * per,
                g * rows_of_group,
                diagonal,
            )

    attend_stretch(me, 1, diagonal=True)
    for copy in locals_:
        copy.wait()
    attend_cache(me)

    def across(k):
        low, high = me - 2 * k + 1 - 2 * i, me + 2 * k + 1 - 2 * i

        @pl.when(o - k >= 0)
        def _():
            for which in (CK, CV, SK, SV):
                relay(which, low, ACROSS).wait_recv()
            attend_cache(low)
            attend_stretch((o - k) * 2, 2)

        @pl.when(o + k < outer)
        def _():
            for which in (CK, CV):
                relay(which, high, ACROSS).wait_recv()
            attend_cache(high)

    partner = me + 1 - 2 * i
    odd = o % 2

    def crosses(which, k, parity):
        return (k > 1) | (odd != parity) | (which != CV)

    def lend(action):
        @pl.when(odd == 0)
        def _():
            action(relay(CV, partner, UP))

        @pl.when(odd == 1)
        def _():
            action(relay(CV, partner, DOWN))

    def step(k, carry):
        low, high = me - 2 * k, me + 2 * k

        def pass_up(*arrays):
            @pl.when(o - k >= 0)
            def _():
                for which in arrays:
                    relay(which, low, UP).wait_recv()

                    @pl.when(o < outer - 1)
                    def _():
                        relay(which, low, UP).start()

                    @pl.when(crosses(which, k, 1))
                    def _():
                        relay(which, low, ACROSS).start()

        def pass_down(*arrays):
            @pl.when(o + k < outer)
            def _():
                for which in arrays:
                    relay(which, high, DOWN).wait_recv()

                    @pl.when(o > 0)
                    def _():
                        relay(which, high, DOWN).start()

                    @pl.when(crosses(which, k, 0))
                    def _():
                        relay(which, high, ACROSS).start()

        pass_up(CK)
        pass_down(CK)
        pass_up(CV)
        pass_down(CV)
        @pl.when(k == 1)
        def _():
            relay(CV, partner, ACROSS).wait_recv()
            lend(lambda copy: copy.start())

        pass_up(SK, SV)

        @pl.when(k > 1)
        def _():
            across(k - 1)

        @pl.when(k == 1)
        def _():
            relay(CK, partner, ACROSS).wait_recv()
            attend_cache(partner)

            @pl.when(i == 1)
            def _():
                for which in (SK, SV):
                    relay(which, partner, ACROSS).wait_recv()
                attend_stretch(partner, 1)

        @pl.when(o - k >= 0)
        def _():
            attend_cache(low)

        @pl.when(o + k < outer)
        def _():
            attend_cache(high)

        return carry

    lax.fori_loop(1, outer, step, 0)
    across(outer - 1)

    for h in range(n):
        rows = slice(h * tok, (h + 1) * tok)
        out_ref[:, h * HEAD : (h + 1) * HEAD] = (acc[rows, :HEAD] / acc[rows, HEAD:]).astype(
            out_ref.dtype
        )

    for copy in shifts:
        copy.wait_send()
    for d in range(1, n):
        table(d).wait_send()
    for which, src in own:
        relay(which, me, ACROSS, src).wait_send()

        @pl.when(o < outer - 1)
        def _():
            relay(which, me, UP, src).wait_send()

        @pl.when(o > 0)
        def _():
            relay(which, me, DOWN, src).wait_send()

    for which in (SK, SV):

        @pl.when(o < outer - 1)
        def _():
            relay(which, me, UP).wait_send()

        @pl.when(i == 0)
        def _():
            relay(which, me, ACROSS).wait_send()

    def drain(k, carry):
        low, high = me - 2 * k, me + 2 * k

        @pl.when(o - k >= 0)
        def _():
            for which in (CK, CV, SK, SV):

                @pl.when(o < outer - 1)
                def _():
                    relay(which, low, UP).wait_send()

                @pl.when(crosses(which, k, 1))
                def _():
                    relay(which, low, ACROSS).wait_send()

        @pl.when(o + k < outer)
        def _():
            for which in (CK, CV):

                @pl.when(o > 0)
                def _():
                    relay(which, high, DOWN).wait_send()

                @pl.when(crosses(which, k, 0))
                def _():
                    relay(which, high, ACROSS).wait_send()

        return carry

    lend(lambda copy: copy.wait_send())
    lax.fori_loop(1, outer, drain, 0)


def solution(mesh):
    layers, n = mesh.shape["section"], mesh.shape["seq"]

    def per_device(queries, keys, values, cache_keys, cache_values, vertical, count, slash):
        tok, wide = queries.shape[1:]
        kv_wide = keys.shape[2]
        part = cache_keys.shape[2]
        per = tok // BLK
        dtype = queries.dtype
        rows = n * tok
        anywhere = pl.BlockSpec(memory_space=pltpu.HBM)
        scalars = pl.BlockSpec(memory_space=pltpu.SMEM)
        keys_all = GROUP * part + n * tok
        result = pl.pallas_call(
            functools.partial(kernel, layers, n),
            out_shape=jax.ShapeDtypeStruct((tok, wide), dtype),
            in_specs=[anywhere] * 5 + [scalars] * 3,
            out_specs=pl.BlockSpec(memory_space=pltpu.VMEM),
            scratch_shapes=[
                pltpu.VMEM((n, part, HEAD), dtype),
                pltpu.VMEM((n, part, HEAD), dtype),
                pltpu.VMEM((n, tok, kv_wide), dtype),
                pltpu.VMEM((n, tok, kv_wide), dtype),
                pltpu.VMEM((tok, wide), dtype),
                pltpu.VMEM((n * per, 1, LANES), jnp.float32),
                pltpu.VMEM((n, per, 1, LANES), jnp.float32),
                pltpu.VMEM((rows, 2 * HEAD), dtype),
                pltpu.VMEM((rows, 2 * HEAD), jnp.float32),
                pltpu.VMEM((rows, LANES), jnp.float32),
                pltpu.SemaphoreType.DMA((2,)),
                pltpu.SemaphoreType.DMA((3,)),
                pltpu.SemaphoreType.DMA,
                pltpu.SemaphoreType.DMA((3, 4, n)),
                pltpu.SemaphoreType.DMA((4, n)),
                pltpu.SemaphoreType.DMA((n,)),
                pltpu.SemaphoreType.DMA((n,)),
            ],
            compiler_params=pltpu.CompilerParams(
                collective_id=0, has_side_effects=True, vmem_limit_bytes=63 * 2**20
            ),
            cost_estimate=pl.CostEstimate(
                flops=4 * rows * keys_all * HEAD,
                bytes_accessed=2 * rows * HEAD * 4,
                transcendentals=rows * keys_all,
            ),
        )(
            queries[0],
            keys[0],
            values[0],
            cache_keys[0, 0],
            cache_values[0, 0],
            vertical[0],
            count,
            slash[0],
        )
        return result[None]

    return jax.shard_map(
        per_device,
        mesh=mesh,
        in_specs=(
            P("section", "seq", None),
            P("section", "seq", None),
            P("section", "seq", None),
            P("section", "seq", None, None),
            P("section", "seq", None, None),
            P("section", "seq", None),
            P("section", "seq"),
            P("section", "seq", None),
        ),
        out_specs=P("section", "seq", None),
        check_vma=False,
    )
```

```python
import functools
import math

import jax
import jax.numpy as jnp
from jax import lax
from jax.experimental import pallas as pl
from jax.experimental.pallas import tpu as pltpu
from jax.sharding import PartitionSpec as P

HEAD = 128
GROUP = 8
BLK = 64
NVMAX = 32
NS = 11
LANES = 128
MASKED = -1e30
MESH = pl.DeviceIdType.MESH
UP, DOWN, ACROSS = 0, 1, 2
CK, CV, SK, SV = 0, 1, 2, 3


def kernel(
    layers,
    n,
    q_hbm,
    k_hbm,
    v_hbm,
    ck_hbm,
    cv_hbm,
    vert_ref,
    count_ref,
    slash_ref,
    out_ref,
    ckbuf,
    cvbuf,
    skbuf,
    svbuf,
    qbuf,
    tabs,
    tabr,
    qaug,
    acc,
    top,
    local_sem,
    shift_send,
    q_recv,
    send_sem,
    recv_sem,
    tab_send,
    tab_recv,
):
    tok = qbuf.shape[0]
    part = ckbuf.shape[1]
    kvh = skbuf.shape[2] // HEAD
    per = tok // BLK
    ncb = GROUP * part // BLK
    nqb = n * per
    rows_of_group = GROUP * tok
    tile = min(4 * tok, rows_of_group)
    outer = n // 2
    sec = lax.axis_index("section")
    me = lax.axis_index("seq")
    o, i = me // 2, me % 2
    after, before = lax.rem(sec + 1, layers), lax.rem(sec + layers - 1, layers)
    scale = math.log2(math.e) / math.sqrt(HEAD)

    barrier = pltpu.get_barrier_semaphore()
    for d in range(1, n):
        pl.semaphore_signal(
            barrier, inc=1, device_id={"seq": lax.rem(me + d, n)}, device_id_type=MESH
        )
    for other in (after, before):
        pl.semaphore_signal(barrier, inc=1, device_id={"section": other}, device_id_type=MESH)
    pl.semaphore_wait(barrier, n + 1)

    bufs = (ckbuf, cvbuf, skbuf, svbuf)
    target = (me + 2, me - 2, me + 1 - 2 * i)

    def relay(which, slot, way, src=None):
        dst = bufs[which].at[slot]
        return pltpu.make_async_remote_copy(
            src_ref=dst if src is None else src,
            dst_ref=dst,
            send_sem=send_sem.at[way, which, slot],
            recv_sem=recv_sem.at[which, slot],
            device_id={"seq": target[way]},
            device_id_type=MESH,
        )

    def shift(src, dst, index, recv):
        return pltpu.make_async_remote_copy(
            src_ref=src,
            dst_ref=dst,
            send_sem=shift_send.at[index],
            recv_sem=recv,
            device_id={"section": after},
            device_id_type=MESH,
        )

    shifts = (
        shift(k_hbm, skbuf.at[me], 0, recv_sem.at[SK, me]),
        shift(v_hbm, svbuf.at[me], 1, recv_sem.at[SV, me]),
        shift(q_hbm, qbuf, 2, q_recv),
    )
    for copy in shifts:
        copy.start()
    own = ((CK, ck_hbm), (CV, cv_hbm))
    for which, src in own:
        relay(which, me, ACROSS, src).start()

        @pl.when(o < outer - 1)
        def _():
            relay(which, me, UP, src).start()

        @pl.when(o > 0)
        def _():
            relay(which, me, DOWN, src).start()

    locals_ = [
        pltpu.make_async_copy(src, bufs[which].at[me], local_sem.at[which]) for which, src in own
    ]
    for copy in locals_:
        copy.start()

    lane = lax.broadcasted_iota(jnp.int32, (1, LANES), 1)
    count = count_ref[0, 0]
    hit = lane < 0
    for slot in range(NVMAX):
        hit = hit | (lane == jnp.where(slot < count, vert_ref[0, slot], -1))
    listed = jnp.where(hit, 1, 0)
    offsets = [slash_ref[0, j] for j in range(NS)]

    def fill(b, carry):
        diagonal = ncb + b
        found = (listed > 0) | (lane == diagonal)
        for off in offsets:
            found = found | (lane == diagonal - off)
        tabs[b] = jnp.where(found, 0.0, MASKED)
        return carry

    lax.fori_loop(0, nqb, fill, 0)

    def table(d):
        to = lax.rem(me + d, n)
        return pltpu.make_async_remote_copy(
            src_ref=tabs.at[pl.ds(to * per, per)],
            dst_ref=tabr.at[me],
            send_sem=tab_send.at[d],
            recv_sem=tab_recv.at[me],
            device_id={"seq": to},
            device_id_type=MESH,
        )

    for d in range(1, n):
        table(d).start()
    tabr[me] = tabs[pl.ds(me * per, per)]

    for which in (SK, SV):
        relay(which, me, UP).wait_recv()

        @pl.when(o < outer - 1)
        def _():
            relay(which, me, UP).start()

        @pl.when(i == 0)
        def _():
            relay(which, me, ACROSS).start()

    def attend(keys, values, first_block, base, diagonal=False):
        width = keys.shape[0]
        block = lax.broadcasted_iota(jnp.int32, (width, LANES), 0) // BLK + first_block
        mark = lax.broadcasted_iota(jnp.int32, (width, LANES), 1) == block
        keys = jnp.concatenate([keys, jnp.where(mark, 1.0, 0.0).astype(jnp.bfloat16)], axis=1)
        values = jnp.concatenate([values, jnp.ones((width, LANES), jnp.bfloat16)], axis=1)
        span = width // LANES

        def scores_of(rows):
            scores = lax.dot_general(
                qaug[rows, :], keys, (((1,), (1,)), ((), ())), preferred_element_type=jnp.float32
            )
            if diagonal:
                token = lax.rem(lax.broadcasted_iota(jnp.int32, (tile, width), 0), tok)
                key = lax.broadcasted_iota(jnp.int32, (tile, width), 1)
                scores = jnp.where(key <= token, scores, MASKED)
            return scores

        def update(rows, scores):
            high = jnp.broadcast_to(jnp.max(scores, axis=1, keepdims=True), (tile, LANES))
            if not diagonal:
                old = top[rows, :]
                high = jnp.maximum(old, high)
            top[rows, :] = high
            wide = jnp.concatenate([high] * span, axis=1)
            weights = jnp.exp2((scores - wide) * scale).astype(jnp.bfloat16)
            fresh = jnp.dot(weights, values, preferred_element_type=jnp.float32)
            if diagonal:
                acc[rows, :] = fresh
            else:
                factor = jnp.exp2((old - high) * scale)
                acc[rows, :] = acc[rows, :] * jnp.concatenate([factor] * 2, axis=1) + fresh

        spans = [
            pl.ds(base + t * tile if kvh == 1 else pl.multiple_of(base + t * tile, tile), tile)
            for t in range(rows_of_group // tile)
        ]
        ahead = scores_of(spans[0])
        for t, rows in enumerate(spans):
            scores = ahead
            if t + 1 < len(spans):
                ahead = scores_of(spans[t + 1])
            update(rows, scores)

    def attend_cache(slot):
        attend(
            ckbuf[slot],
            cvbuf[slot],
            lax.rem(slot, GROUP) * (part // BLK),
            0 if kvh == 1 else slot // GROUP * rows_of_group,
        )

    def attend_stretch(slot, slots, diagonal=False):
        for g in range(kvh):
            keys = skbuf[pl.ds(slot, slots), :, g * HEAD : (g + 1) * HEAD]
            values = svbuf[pl.ds(slot, slots), :, g * HEAD : (g + 1) * HEAD]
            attend(
                keys.reshape(slots * tok, HEAD),
                values.reshape(slots * tok, HEAD),
                ncb + slot * per,
                g * rows_of_group,
                diagonal,
            )

    def across(k):
        low, high = me - 2 * k + 1 - 2 * i, me + 2 * k + 1 - 2 * i

        @pl.when(o - k >= 0)
        def _():
            for which in (CK, CV, SK, SV):
                relay(which, low, ACROSS).wait_recv()
            attend_cache(low)
            attend_stretch((o - k) * 2, 2)

        @pl.when(o + k < outer)
        def _():
            for which in (CK, CV):
                relay(which, high, ACROSS).wait_recv()
            attend_cache(high)

    partner = me + 1 - 2 * i
    odd = o % 2

    def crosses(which, k, parity):
        return (k > 1) | (odd != parity) | (which != CV)

    def lend(action):
        @pl.when(odd == 0)
        def _():
            action(relay(CV, partner, UP))

        @pl.when(odd == 1)
        def _():
            action(relay(CV, partner, DOWN))

    def pass_up(k, *arrays):
        low = me - 2 * k

        @pl.when(o - k >= 0)
        def _():
            for which in arrays:
                relay(which, low, UP).wait_recv()

                @pl.when(o < outer - 1)
                def _():
                    relay(which, low, UP).start()

                @pl.when(crosses(which, k, 1))
                def _():
                    relay(which, low, ACROSS).start()

    def pass_down(k, *arrays):
        high = me + 2 * k

        @pl.when(o + k < outer)
        def _():
            for which in arrays:
                relay(which, high, DOWN).wait_recv()

                @pl.when(o > 0)
                def _():
                    relay(which, high, DOWN).start()

                @pl.when(crosses(which, k, 0))
                def _():
                    relay(which, high, ACROSS).start()

    def along(k):
        @pl.when(o - k >= 0)
        def _():
            attend_cache(me - 2 * k)

        @pl.when(o + k < outer)
        def _():
            attend_cache(me + 2 * k)

    pass_up(1, CK)
    pass_down(1, CK)
    shifts[2].wait_recv()
    for d in range(1, n):
        src = lax.rem(me + d, n)
        pltpu.make_async_remote_copy(
            src_ref=tabs.at[pl.ds(0, per)],
            dst_ref=tabr.at[src],
            send_sem=tab_send.at[d],
            recv_sem=tab_recv.at[src],
            device_id={"seq": src},
            device_id_type=MESH,
        ).wait_recv()
    for h in range(n):
        qaug[h * tok : (h + 1) * tok, :HEAD] = qbuf[:, h * HEAD : (h + 1) * HEAD]
        for j in range(per):
            qaug[h * tok + j * BLK : h * tok + (j + 1) * BLK, HEAD:] = jnp.broadcast_to(
                tabr[h, j].astype(jnp.bfloat16), (BLK, LANES)
            )

    pass_up(1, CV)
    pass_down(1, CV)
    attend_stretch(me, 1, diagonal=True)
    relay(CV, partner, ACROSS).wait_recv()
    lend(lambda copy: copy.start())
    pass_up(1, SK, SV)
    for copy in locals_:
        copy.wait()
    attend_cache(me)
    relay(CK, partner, ACROSS).wait_recv()
    attend_cache(partner)

    @pl.when(i == 1)
    def _():
        for which in (SK, SV):
            relay(which, partner, ACROSS).wait_recv()
        attend_stretch(partner, 1)

    def step(k, carry):
        along(k - 1)
        pass_up(k, CK)
        pass_down(k, CK)
        pass_up(k, CV)
        pass_down(k, CV)
        pass_up(k, SK, SV)
        across(k - 1)
        return carry

    lax.fori_loop(2, outer, step, 0)
    along(outer - 1)
    across(outer - 1)

    for h in range(n):
        rows = slice(h * tok, (h + 1) * tok)
        out_ref[:, h * HEAD : (h + 1) * HEAD] = (acc[rows, :HEAD] / acc[rows, HEAD:]).astype(
            out_ref.dtype
        )

    for copy in shifts:
        copy.wait_send()
    for d in range(1, n):
        table(d).wait_send()
    for which, src in own:
        relay(which, me, ACROSS, src).wait_send()

        @pl.when(o < outer - 1)
        def _():
            relay(which, me, UP, src).wait_send()

        @pl.when(o > 0)
        def _():
            relay(which, me, DOWN, src).wait_send()

    for which in (SK, SV):

        @pl.when(o < outer - 1)
        def _():
            relay(which, me, UP).wait_send()

        @pl.when(i == 0)
        def _():
            relay(which, me, ACROSS).wait_send()

    def drain(k, carry):
        low, high = me - 2 * k, me + 2 * k

        @pl.when(o - k >= 0)
        def _():
            for which in (CK, CV, SK, SV):

                @pl.when(o < outer - 1)
                def _():
                    relay(which, low, UP).wait_send()

                @pl.when(crosses(which, k, 1))
                def _():
                    relay(which, low, ACROSS).wait_send()

        @pl.when(o + k < outer)
        def _():
            for which in (CK, CV):

                @pl.when(o > 0)
                def _():
                    relay(which, high, DOWN).wait_send()

                @pl.when(crosses(which, k, 0))
                def _():
                    relay(which, high, ACROSS).wait_send()

        return carry

    lend(lambda copy: copy.wait_send())
    lax.fori_loop(1, outer, drain, 0)


def solution(mesh):
    layers, n = mesh.shape["section"], mesh.shape["seq"]

    def per_device(queries, keys, values, cache_keys, cache_values, vertical, count, slash):
        tok, wide = queries.shape[1:]
        kv_wide = keys.shape[2]
        part = cache_keys.shape[2]
        per = tok // BLK
        dtype = queries.dtype
        rows = n * tok
        anywhere = pl.BlockSpec(memory_space=pltpu.HBM)
        scalars = pl.BlockSpec(memory_space=pltpu.SMEM)
        keys_all = GROUP * part + n * tok
        result = pl.pallas_call(
            functools.partial(kernel, layers, n),
            out_shape=pltpu.VMEM((tok, wide), dtype),
            in_specs=[anywhere] * 5 + [scalars] * 3,
            out_specs=pl.BlockSpec(memory_space=pltpu.VMEM),
            scratch_shapes=[
                pltpu.VMEM((n, part, HEAD), dtype),
                pltpu.VMEM((n, part, HEAD), dtype),
                pltpu.VMEM((n, tok, kv_wide), dtype),
                pltpu.VMEM((n, tok, kv_wide), dtype),
                pltpu.VMEM((tok, wide), dtype),
                pltpu.VMEM((n * per, 1, LANES), jnp.float32),
                pltpu.VMEM((n, per, 1, LANES), jnp.float32),
                pltpu.VMEM((rows, 2 * HEAD), dtype),
                pltpu.VMEM((rows, 2 * HEAD), jnp.float32),
                pltpu.VMEM((rows, LANES), jnp.float32),
                pltpu.SemaphoreType.DMA((2,)),
                pltpu.SemaphoreType.DMA((3,)),
                pltpu.SemaphoreType.DMA,
                pltpu.SemaphoreType.DMA((3, 4, n)),
                pltpu.SemaphoreType.DMA((4, n)),
                pltpu.SemaphoreType.DMA((n,)),
                pltpu.SemaphoreType.DMA((n,)),
            ],
            compiler_params=pltpu.CompilerParams(
                collective_id=0, has_side_effects=True, vmem_limit_bytes=60 * 2**20
            ),
            cost_estimate=pl.CostEstimate(
                flops=4 * rows * keys_all * HEAD,
                bytes_accessed=2 * rows * HEAD * 4,
                transcendentals=rows * keys_all,
            ),
        )(
            queries[0],
            keys[0],
            values[0],
            cache_keys[0, 0],
            cache_values[0, 0],
            vertical[0],
            count,
            slash[0],
        )
        return result[None]

    return jax.shard_map(
        per_device,
        mesh=mesh,
        in_specs=(
            P("section", "seq", None),
            P("section", "seq", None),
            P("section", "seq", None),
            P("section", "seq", None, None),
            P("section", "seq", None, None),
            P("section", "seq", None),
            P("section", "seq"),
            P("section", "seq", None),
        ),
        out_specs=P("section", "seq", None),
        check_vma=False,
    )
```

```python
import functools
import math

import jax
import jax.numpy as jnp
from jax import lax
from jax.experimental import pallas as pl
from jax.experimental.pallas import tpu as pltpu
from jax.sharding import PartitionSpec as P

HEAD = 128
GROUP = 8
BLK = 64
NVMAX = 32
NS = 11
LANES = 128
MASKED = -1e30
MESH = pl.DeviceIdType.MESH
UP, DOWN, ACROSS = 0, 1, 2
CK, CV, SK, SV = 0, 1, 2, 3


def kernel(
    layers,
    n,
    q_hbm,
    k_hbm,
    v_hbm,
    ck_hbm,
    cv_hbm,
    vert_ref,
    count_ref,
    slash_ref,
    out_ref,
    ckbuf,
    cvbuf,
    skbuf,
    svbuf,
    qbuf,
    tabs,
    tabr,
    qaug,
    acc,
    top,
    local_sem,
    shift_send,
    q_recv,
    send_sem,
    recv_sem,
    tab_send,
    tab_recv,
):
    tok = qbuf.shape[0]
    part = ckbuf.shape[1]
    kvh = skbuf.shape[2] // HEAD
    per = tok // BLK
    ncb = GROUP * part // BLK
    nqb = n * per
    rows_of_group = GROUP * tok
    tile = min(4 * tok, rows_of_group)
    outer = n // 2
    sec = lax.axis_index("section")
    me = lax.axis_index("seq")
    o, i = me // 2, me % 2
    after, before = lax.rem(sec + 1, layers), lax.rem(sec + layers - 1, layers)
    scale = math.log2(math.e) / math.sqrt(HEAD)

    barrier = pltpu.get_barrier_semaphore()
    for d in range(1, n):
        pl.semaphore_signal(
            barrier, inc=1, device_id={"seq": lax.rem(me + d, n)}, device_id_type=MESH
        )
    for other in (after, before):
        pl.semaphore_signal(barrier, inc=1, device_id={"section": other}, device_id_type=MESH)
    pl.semaphore_wait(barrier, n + 1)

    bufs = (ckbuf, cvbuf, skbuf, svbuf)
    target = (me + 2, me - 2, me + 1 - 2 * i)

    def relay(which, slot, way, src=None):
        dst = bufs[which].at[slot]
        return pltpu.make_async_remote_copy(
            src_ref=dst if src is None else src,
            dst_ref=dst,
            send_sem=send_sem.at[way, which, slot],
            recv_sem=recv_sem.at[which, slot],
            device_id={"seq": target[way]},
            device_id_type=MESH,
        )

    def shift(src, dst, index, recv):
        return pltpu.make_async_remote_copy(
            src_ref=src,
            dst_ref=dst,
            send_sem=shift_send.at[index],
            recv_sem=recv,
            device_id={"section": after},
            device_id_type=MESH,
        )

    shifts = (
        shift(k_hbm, skbuf.at[me], 0, recv_sem.at[SK, me]),
        shift(v_hbm, svbuf.at[me], 1, recv_sem.at[SV, me]),
        shift(q_hbm, qbuf, 2, q_recv),
    )
    for copy in shifts:
        copy.start()
    own = ((CK, ck_hbm), (CV, cv_hbm))
    for which, src in own:
        relay(which, me, ACROSS, src).start()

        @pl.when(o < outer - 1)
        def _():
            relay(which, me, UP, src).start()

        @pl.when(o > 0)
        def _():
            relay(which, me, DOWN, src).start()

    locals_ = [
        pltpu.make_async_copy(src, bufs[which].at[me], local_sem.at[which]) for which, src in own
    ]
    for copy in locals_:
        copy.start()

    lane = lax.broadcasted_iota(jnp.int32, (1, LANES), 1)
    count = count_ref[0, 0]
    hit = lane < 0
    for slot in range(NVMAX):
        hit = hit | (lane == jnp.where(slot < count, vert_ref[0, slot], -1))
    listed = jnp.where(hit, 1, 0)
    offsets = [slash_ref[0, j] for j in range(NS)]

    def fill(b, carry):
        diagonal = ncb + b
        found = (listed > 0) | (lane == diagonal)
        for off in offsets:
            found = found | (lane == diagonal - off)
        tabs[b] = jnp.where(found, 0.0, MASKED)
        return carry

    lax.fori_loop(0, nqb, fill, 0)

    def table(d):
        to = lax.rem(me + d, n)
        return pltpu.make_async_remote_copy(
            src_ref=tabs.at[pl.ds(to * per, per)],
            dst_ref=tabr.at[me],
            send_sem=tab_send.at[d],
            recv_sem=tab_recv.at[me],
            device_id={"seq": to},
            device_id_type=MESH,
        )

    for d in range(1, n):
        table(d).start()
    tabr[me] = tabs[pl.ds(me * per, per)]

    for which in (SK, SV):
        relay(which, me, UP).wait_recv()

        @pl.when(o < outer - 1)
        def _():
            relay(which, me, UP).start()

        @pl.when(i == 0)
        def _():
            relay(which, me, ACROSS).start()

    def attend(keys, values, first_block, base, diagonal=False):
        width = keys.shape[0]
        block = lax.broadcasted_iota(jnp.int32, (width, LANES), 0) // BLK + first_block
        mark = lax.broadcasted_iota(jnp.int32, (width, LANES), 1) == block
        keys = jnp.concatenate([keys, jnp.where(mark, 1.0, 0.0).astype(jnp.bfloat16)], axis=1)
        values = jnp.concatenate([values, jnp.ones((width, LANES), jnp.bfloat16)], axis=1)
        span = width // LANES

        def scores_of(rows):
            scores = lax.dot_general(
                qaug[rows, :], keys, (((1,), (1,)), ((), ())), preferred_element_type=jnp.float32
            )
            if diagonal:
                token = lax.rem(lax.broadcasted_iota(jnp.int32, (tile, width), 0), tok)
                key = lax.broadcasted_iota(jnp.int32, (tile, width), 1)
                scores = jnp.where(key <= token, scores, MASKED)
            return scores

        def update(rows, scores):
            high = jnp.broadcast_to(jnp.max(scores, axis=1, keepdims=True), (tile, LANES))
            if not diagonal:
                old = top[rows, :]
                high = jnp.maximum(old, high)
            top[rows, :] = high
            wide = jnp.concatenate([high] * span, axis=1)
            weights = jnp.exp2((scores - wide) * scale).astype(jnp.bfloat16)
            fresh = jnp.dot(weights, values, preferred_element_type=jnp.float32)
            if diagonal:
                acc[rows, :] = fresh
            else:
                factor = jnp.exp2((old - high) * scale)
                acc[rows, :] = acc[rows, :] * jnp.concatenate([factor] * 2, axis=1) + fresh

        spans = [
            pl.ds(base + t * tile if kvh == 1 else pl.multiple_of(base + t * tile, tile), tile)
            for t in range(rows_of_group // tile)
        ]
        ahead = scores_of(spans[0])
        for t, rows in enumerate(spans):
            scores = ahead
            if t + 1 < len(spans):
                ahead = scores_of(spans[t + 1])
            update(rows, scores)

    def attend_cache(slot):
        attend(
            ckbuf[slot],
            cvbuf[slot],
            lax.rem(slot, GROUP) * (part // BLK),
            0 if kvh == 1 else slot // GROUP * rows_of_group,
        )

    def attend_stretch(slot, slots, diagonal=False):
        for g in range(kvh):
            keys = skbuf[pl.ds(slot, slots), :, g * HEAD : (g + 1) * HEAD]
            values = svbuf[pl.ds(slot, slots), :, g * HEAD : (g + 1) * HEAD]
            attend(
                keys.reshape(slots * tok, HEAD),
                values.reshape(slots * tok, HEAD),
                ncb + slot * per,
                g * rows_of_group,
                diagonal,
            )

    def across(k):
        low, high = me - 2 * k + 1 - 2 * i, me + 2 * k + 1 - 2 * i

        @pl.when(o - k >= 0)
        def _():
            for which in (SK, SV):
                relay(which, low, ACROSS).wait_recv()
            attend_stretch((o - k) * 2, 2)
            relay(CK, low, ACROSS).wait_recv()

            @pl.when(o != k)
            def _():
                relay(CV, low, ACROSS).wait_recv()

            attend_cache(low)

        @pl.when(o + k < outer)
        def _():
            relay(CK, high, ACROSS).wait_recv()

            @pl.when(o + k != outer - 1)
            def _():
                relay(CV, high, ACROSS).wait_recv()

            attend_cache(high)

    partner = me + 1 - 2 * i
    lent_low, lent_high = 1 - i, 2 * (outer - 1) + 1 - i

    def lend(action):
        @pl.when(o == 0)
        def _():
            action(relay(CV, partner, UP))

        @pl.when(o == outer - 1)
        def _():
            action(relay(CV, partner, DOWN))

    def pass_lent(k):
        @pl.when(o == k)
        def _():
            relay(CV, lent_low, UP).wait_recv()

            @pl.when(o < outer - 1)
            def _():
                relay(CV, lent_low, UP).start()

        @pl.when(o + k == outer - 1)
        def _():
            relay(CV, lent_high, DOWN).wait_recv()

            @pl.when(o > 0)
            def _():
                relay(CV, lent_high, DOWN).start()

    def pass_up(k, *arrays):
        low = me - 2 * k

        @pl.when(o - k >= 0)
        def _():
            for which in arrays:
                relay(which, low, UP).wait_recv()

                @pl.when(o < outer - 1)
                def _():
                    relay(which, low, UP).start()

                @pl.when((which != CV) | (o != k))
                def _():
                    relay(which, low, ACROSS).start()

    def pass_down(k, *arrays):
        high = me + 2 * k

        @pl.when(o + k < outer)
        def _():
            for which in arrays:
                relay(which, high, DOWN).wait_recv()

                @pl.when(o > 0)
                def _():
                    relay(which, high, DOWN).start()

                @pl.when((which != CV) | (o + k != outer - 1))
                def _():
                    relay(which, high, ACROSS).start()

    def along(k):
        @pl.when(o - k >= 0)
        def _():
            attend_cache(me - 2 * k)

        @pl.when(o + k < outer)
        def _():
            attend_cache(me + 2 * k)

    pass_up(1, CK)
    pass_down(1, CK)
    shifts[2].wait_recv()
    for d in range(1, n):
        src = lax.rem(me + d, n)
        pltpu.make_async_remote_copy(
            src_ref=tabs.at[pl.ds(0, per)],
            dst_ref=tabr.at[src],
            send_sem=tab_send.at[d],
            recv_sem=tab_recv.at[src],
            device_id={"seq": src},
            device_id_type=MESH,
        ).wait_recv()
    for h in range(n):
        qaug[h * tok : (h + 1) * tok, :HEAD] = qbuf[:, h * HEAD : (h + 1) * HEAD]
        for j in range(per):
            qaug[h * tok + j * BLK : h * tok + (j + 1) * BLK, HEAD:] = jnp.broadcast_to(
                tabr[h, j].astype(jnp.bfloat16), (BLK, LANES)
            )

    pass_up(1, CV)
    pass_down(1, CV)
    attend_stretch(me, 1, diagonal=True)
    relay(CV, partner, ACROSS).wait_recv()
    lend(lambda copy: copy.start())
    pass_up(1, SK, SV)
    for copy in locals_:
        copy.wait()
    attend_cache(me)
    relay(CK, partner, ACROSS).wait_recv()
    attend_cache(partner)

    @pl.when(i == 1)
    def _():
        for which in (SK, SV):
            relay(which, partner, ACROSS).wait_recv()
        attend_stretch(partner, 1)

    def step(k, carry):
        along(k - 1)
        pass_lent(k - 1)
        pass_up(k, CK)
        pass_down(k, CK)
        pass_up(k, SK, SV)
        pass_up(k, CV)
        pass_down(k, CV)
        across(k - 1)
        return carry

    lax.fori_loop(2, outer, step, 0)
    along(outer - 1)
    pass_lent(outer - 1)
    across(outer - 1)

    for h in range(n):
        rows = slice(h * tok, (h + 1) * tok)
        out_ref[:, h * HEAD : (h + 1) * HEAD] = (acc[rows, :HEAD] / acc[rows, HEAD:]).astype(
            out_ref.dtype
        )

    for copy in shifts:
        copy.wait_send()
    for d in range(1, n):
        table(d).wait_send()
    for which, src in own:
        relay(which, me, ACROSS, src).wait_send()

        @pl.when(o < outer - 1)
        def _():
            relay(which, me, UP, src).wait_send()

        @pl.when(o > 0)
        def _():
            relay(which, me, DOWN, src).wait_send()

    for which in (SK, SV):

        @pl.when(o < outer - 1)
        def _():
            relay(which, me, UP).wait_send()

        @pl.when(i == 0)
        def _():
            relay(which, me, ACROSS).wait_send()

    def drain(k, carry):
        low, high = me - 2 * k, me + 2 * k

        @pl.when(o - k >= 0)
        def _():
            for which in (CK, CV, SK, SV):

                @pl.when(o < outer - 1)
                def _():
                    relay(which, low, UP).wait_send()

                @pl.when((which != CV) | (o != k))
                def _():
                    relay(which, low, ACROSS).wait_send()

        @pl.when(o + k < outer)
        def _():
            for which in (CK, CV):

                @pl.when(o > 0)
                def _():
                    relay(which, high, DOWN).wait_send()

                @pl.when((which != CV) | (o + k != outer - 1))
                def _():
                    relay(which, high, ACROSS).wait_send()

        return carry

    lend(lambda copy: copy.wait_send())

    @pl.when((o > 0) & (o < outer - 1))
    def _():
        relay(CV, lent_low, UP).wait_send()
        relay(CV, lent_high, DOWN).wait_send()

    lax.fori_loop(1, outer, drain, 0)


def solution(mesh):
    layers, n = mesh.shape["section"], mesh.shape["seq"]

    def per_device(queries, keys, values, cache_keys, cache_values, vertical, count, slash):
        tok, wide = queries.shape[1:]
        kv_wide = keys.shape[2]
        part = cache_keys.shape[2]
        per = tok // BLK
        dtype = queries.dtype
        rows = n * tok
        anywhere = pl.BlockSpec(memory_space=pltpu.HBM)
        scalars = pl.BlockSpec(memory_space=pltpu.SMEM)
        keys_all = GROUP * part + n * tok
        result = pl.pallas_call(
            functools.partial(kernel, layers, n),
            out_shape=pltpu.VMEM((tok, wide), dtype),
            in_specs=[anywhere] * 5 + [scalars] * 3,
            out_specs=pl.BlockSpec(memory_space=pltpu.VMEM),
            scratch_shapes=[
                pltpu.VMEM((n, part, HEAD), dtype),
                pltpu.VMEM((n, part, HEAD), dtype),
                pltpu.VMEM((n, tok, kv_wide), dtype),
                pltpu.VMEM((n, tok, kv_wide), dtype),
                pltpu.VMEM((tok, wide), dtype),
                pltpu.VMEM((n * per, 1, LANES), jnp.float32),
                pltpu.VMEM((n, per, 1, LANES), jnp.float32),
                pltpu.VMEM((rows, 2 * HEAD), dtype),
                pltpu.VMEM((rows, 2 * HEAD), jnp.float32),
                pltpu.VMEM((rows, LANES), jnp.float32),
                pltpu.SemaphoreType.DMA((2,)),
                pltpu.SemaphoreType.DMA((3,)),
                pltpu.SemaphoreType.DMA,
                pltpu.SemaphoreType.DMA((3, 4, n)),
                pltpu.SemaphoreType.DMA((4, n)),
                pltpu.SemaphoreType.DMA((n,)),
                pltpu.SemaphoreType.DMA((n,)),
            ],
            compiler_params=pltpu.CompilerParams(
                collective_id=0, has_side_effects=True, vmem_limit_bytes=60 * 2**20
            ),
            cost_estimate=pl.CostEstimate(
                flops=4 * rows * keys_all * HEAD,
                bytes_accessed=2 * rows * HEAD * 4,
                transcendentals=rows * keys_all,
            ),
        )(
            queries[0],
            keys[0],
            values[0],
            cache_keys[0, 0],
            cache_values[0, 0],
            vertical[0],
            count,
            slash[0],
        )
        return result[None]

    return jax.shard_map(
        per_device,
        mesh=mesh,
        in_specs=(
            P("section", "seq", None),
            P("section", "seq", None),
            P("section", "seq", None),
            P("section", "seq", None, None),
            P("section", "seq", None, None),
            P("section", "seq", None),
            P("section", "seq"),
            P("section", "seq", None),
        ),
        out_specs=P("section", "seq", None),
        check_vma=False,
    )
```

```python
import functools
import math

import jax
import jax.numpy as jnp
from jax import lax
from jax.experimental import pallas as pl
from jax.experimental.pallas import tpu as pltpu
from jax.sharding import PartitionSpec as P

HEAD = 128
GROUP = 8
BLK = 64
NVMAX = 32
NS = 11
LANES = 128
MASKED = -1e30
MESH = pl.DeviceIdType.MESH
UP, DOWN, ACROSS = 0, 1, 2
CK, CV, SK, SV = 0, 1, 2, 3


def kernel(
    layers,
    n,
    q_hbm,
    k_hbm,
    v_hbm,
    ck_hbm,
    cv_hbm,
    vert_ref,
    count_ref,
    slash_ref,
    out_ref,
    ckbuf,
    cvbuf,
    skbuf,
    svbuf,
    qbuf,
    tabs,
    tabr,
    qaug,
    acc,
    top,
    local_sem,
    shift_send,
    q_recv,
    send_sem,
    recv_sem,
    tab_send,
    tab_recv,
):
    tok = qbuf.shape[0]
    part = ckbuf.shape[1]
    kvh = skbuf.shape[2] // HEAD
    per = tok // BLK
    ncb = GROUP * part // BLK
    nqb = n * per
    rows_of_group = GROUP * tok
    tile = min(4 * tok, rows_of_group)
    outer = n // 2
    sec = lax.axis_index("section")
    me = lax.axis_index("seq")
    o, i = me // 2, me % 2
    after, before = lax.rem(sec + 1, layers), lax.rem(sec + layers - 1, layers)
    scale = math.log2(math.e) / math.sqrt(HEAD)

    barrier = pltpu.get_barrier_semaphore()
    for d in range(1, n):
        pl.semaphore_signal(
            barrier, inc=1, device_id={"seq": lax.rem(me + d, n)}, device_id_type=MESH
        )
    for other in (after, before):
        pl.semaphore_signal(barrier, inc=1, device_id={"section": other}, device_id_type=MESH)
    pl.semaphore_wait(barrier, n + 1)

    bufs = (ckbuf, cvbuf, skbuf, svbuf)
    target = (me + 2, me - 2, me + 1 - 2 * i)

    def relay(which, slot, way, src=None):
        dst = bufs[which].at[slot]
        return pltpu.make_async_remote_copy(
            src_ref=dst if src is None else src,
            dst_ref=dst,
            send_sem=send_sem.at[way, which, slot],
            recv_sem=recv_sem.at[which, slot],
            device_id={"seq": target[way]},
            device_id_type=MESH,
        )

    def shift(src, dst, index, recv):
        return pltpu.make_async_remote_copy(
            src_ref=src,
            dst_ref=dst,
            send_sem=shift_send.at[index],
            recv_sem=recv,
            device_id={"section": after},
            device_id_type=MESH,
        )

    shifts = (
        shift(k_hbm, skbuf.at[me], 0, recv_sem.at[SK, me]),
        shift(v_hbm, svbuf.at[me], 1, recv_sem.at[SV, me]),
        shift(q_hbm, qbuf, 2, q_recv),
    )
    for copy in shifts:
        copy.start()
    own = ((CK, ck_hbm), (CV, cv_hbm))
    for which, src in own:
        relay(which, me, ACROSS, src).start()

        @pl.when(o < outer - 1)
        def _():
            relay(which, me, UP, src).start()

        @pl.when(o > 0)
        def _():
            relay(which, me, DOWN, src).start()

    locals_ = [
        pltpu.make_async_copy(src, bufs[which].at[me], local_sem.at[which]) for which, src in own
    ]
    for copy in locals_:
        copy.start()

    lane = lax.broadcasted_iota(jnp.int32, (1, LANES), 1)
    count = count_ref[0, 0]
    hit = lane < 0
    for slot in range(NVMAX):
        hit = hit | (lane == jnp.where(slot < count, vert_ref[0, slot], -1))
    listed = jnp.where(hit, 1, 0)
    offsets = [slash_ref[0, j] for j in range(NS)]

    def fill(b, carry):
        diagonal = ncb + b
        found = (listed > 0) | (lane == diagonal)
        for off in offsets:
            found = found | (lane == diagonal - off)
        tabs[b] = jnp.where(found, 0.0, MASKED)
        return carry

    lax.fori_loop(0, nqb, fill, 0)

    def table(d):
        to = lax.rem(me + d, n)
        return pltpu.make_async_remote_copy(
            src_ref=tabs.at[pl.ds(to * per, per)],
            dst_ref=tabr.at[me],
            send_sem=tab_send.at[d],
            recv_sem=tab_recv.at[me],
            device_id={"seq": to},
            device_id_type=MESH,
        )

    for d in range(1, n):
        table(d).start()
    tabr[me] = tabs[pl.ds(me * per, per)]

    def attend(keys, values, first_block, base, diagonal=False):
        width = keys.shape[0]
        block = lax.broadcasted_iota(jnp.int32, (width, LANES), 0) // BLK + first_block
        mark = lax.broadcasted_iota(jnp.int32, (width, LANES), 1) == block
        keys = jnp.concatenate([keys, jnp.where(mark, 1.0, 0.0).astype(jnp.bfloat16)], axis=1)
        values = jnp.concatenate([values, jnp.ones((width, LANES), jnp.bfloat16)], axis=1)
        span = width // LANES

        def scores_of(rows):
            scores = lax.dot_general(
                qaug[rows, :], keys, (((1,), (1,)), ((), ())), preferred_element_type=jnp.float32
            )
            if diagonal:
                token = lax.rem(lax.broadcasted_iota(jnp.int32, (tile, width), 0), tok)
                key = lax.broadcasted_iota(jnp.int32, (tile, width), 1)
                scores = jnp.where(key <= token, scores, MASKED)
            return scores

        def update(rows, scores):
            high = jnp.broadcast_to(jnp.max(scores, axis=1, keepdims=True), (tile, LANES))
            if not diagonal:
                old = top[rows, :]
                high = jnp.maximum(old, high)
            top[rows, :] = high
            wide = jnp.concatenate([high] * span, axis=1)
            weights = jnp.exp2((scores - wide) * scale).astype(jnp.bfloat16)
            fresh = jnp.dot(weights, values, preferred_element_type=jnp.float32)
            if diagonal:
                acc[rows, :] = fresh
            else:
                factor = jnp.exp2((old - high) * scale)
                acc[rows, :] = acc[rows, :] * jnp.concatenate([factor] * 2, axis=1) + fresh

        spans = [
            pl.ds(base + t * tile if kvh == 1 else pl.multiple_of(base + t * tile, tile), tile)
            for t in range(rows_of_group // tile)
        ]
        ahead = scores_of(spans[0])
        for t, rows in enumerate(spans):
            scores = ahead
            if t + 1 < len(spans):
                ahead = scores_of(spans[t + 1])
            update(rows, scores)

    def attend_cache(slot):
        attend(
            ckbuf[slot],
            cvbuf[slot],
            lax.rem(slot, GROUP) * (part // BLK),
            0 if kvh == 1 else slot // GROUP * rows_of_group,
        )

    def attend_stretch(slot, slots, diagonal=False):
        for g in range(kvh):
            keys = skbuf[pl.ds(slot, slots), :, g * HEAD : (g + 1) * HEAD]
            values = svbuf[pl.ds(slot, slots), :, g * HEAD : (g + 1) * HEAD]
            attend(
                keys.reshape(slots * tok, HEAD),
                values.reshape(slots * tok, HEAD),
                ncb + slot * per,
                g * rows_of_group,
                diagonal,
            )

    def across(k):
        low, high = me - 2 * k + 1 - 2 * i, me + 2 * k + 1 - 2 * i

        @pl.when(o - k >= 0)
        def _():
            for which in (SK, SV):
                relay(which, low, ACROSS).wait_recv()
            attend_stretch((o - k) * 2, 2)
            relay(CK, low, ACROSS).wait_recv()

            @pl.when(o != k)
            def _():
                relay(CV, low, ACROSS).wait_recv()

            attend_cache(low)

        @pl.when(o + k < outer)
        def _():
            relay(CK, high, ACROSS).wait_recv()

            @pl.when(o + k != outer - 1)
            def _():
                relay(CV, high, ACROSS).wait_recv()

            attend_cache(high)

    partner = me + 1 - 2 * i
    lent_low, lent_high = 1 - i, 2 * (outer - 1) + 1 - i

    def lend(action):
        @pl.when(o == 0)
        def _():
            action(relay(CV, partner, UP))

        @pl.when(o == outer - 1)
        def _():
            action(relay(CV, partner, DOWN))

    def pass_lent(k):
        @pl.when(o == k)
        def _():
            relay(CV, lent_low, UP).wait_recv()

            @pl.when(o < outer - 1)
            def _():
                relay(CV, lent_low, UP).start()

        @pl.when(o + k == outer - 1)
        def _():
            relay(CV, lent_high, DOWN).wait_recv()

            @pl.when(o > 0)
            def _():
                relay(CV, lent_high, DOWN).start()

    def pass_up(k, *arrays):
        low = me - 2 * k

        @pl.when(o - k >= 0)
        def _():
            for which in arrays:
                relay(which, low, UP).wait_recv()

                @pl.when(o < outer - 1)
                def _():
                    relay(which, low, UP).start()

                @pl.when((which != CV) | (o != k))
                def _():
                    relay(which, low, ACROSS).start()

    def pass_down(k, *arrays):
        high = me + 2 * k

        @pl.when(o + k < outer)
        def _():
            for which in arrays:
                relay(which, high, DOWN).wait_recv()

                @pl.when(o > 0)
                def _():
                    relay(which, high, DOWN).start()

                @pl.when((which != CV) | (o + k != outer - 1))
                def _():
                    relay(which, high, ACROSS).start()

    def along(k):
        @pl.when(o - k >= 0)
        def _():
            attend_cache(me - 2 * k)

        @pl.when(o + k < outer)
        def _():
            attend_cache(me + 2 * k)

    pass_up(1, CK)
    pass_down(1, CK)
    for which in (SK, SV):
        relay(which, me, UP).wait_recv()

        @pl.when(o < outer - 1)
        def _():
            relay(which, me, UP).start()

        @pl.when(i == 0)
        def _():
            relay(which, me, ACROSS).start()

    pass_up(1, CV)
    pass_down(1, CV)
    shifts[2].wait_recv()
    for d in range(1, n):
        src = lax.rem(me + d, n)
        pltpu.make_async_remote_copy(
            src_ref=tabs.at[pl.ds(0, per)],
            dst_ref=tabr.at[src],
            send_sem=tab_send.at[d],
            recv_sem=tab_recv.at[src],
            device_id={"seq": src},
            device_id_type=MESH,
        ).wait_recv()
    for h in range(n):
        qaug[h * tok : (h + 1) * tok, :HEAD] = qbuf[:, h * HEAD : (h + 1) * HEAD]
        for j in range(per):
            qaug[h * tok + j * BLK : h * tok + (j + 1) * BLK, HEAD:] = jnp.broadcast_to(
                tabr[h, j].astype(jnp.bfloat16), (BLK, LANES)
            )

    attend_stretch(me, 1, diagonal=True)
    relay(CV, partner, ACROSS).wait_recv()
    lend(lambda copy: copy.start())
    pass_up(1, SK, SV)
    for copy in locals_:
        copy.wait()
    attend_cache(me)
    relay(CK, partner, ACROSS).wait_recv()
    attend_cache(partner)

    @pl.when(i == 1)
    def _():
        for which in (SK, SV):
            relay(which, partner, ACROSS).wait_recv()
        attend_stretch(partner, 1)

    def step(k, carry):
        along(k - 1)
        pass_lent(k - 1)
        pass_up(k, CK)
        pass_down(k, CK)
        pass_up(k, SK, SV)
        pass_up(k, CV)
        pass_down(k, CV)
        across(k - 1)
        return carry

    lax.fori_loop(2, outer, step, 0)
    along(outer - 1)
    pass_lent(outer - 1)
    across(outer - 1)

    for h in range(n):
        rows = slice(h * tok, (h + 1) * tok)
        out_ref[:, h * HEAD : (h + 1) * HEAD] = (acc[rows, :HEAD] / acc[rows, HEAD:]).astype(
            out_ref.dtype
        )

    for copy in shifts:
        copy.wait_send()
    for d in range(1, n):
        table(d).wait_send()
    for which, src in own:
        relay(which, me, ACROSS, src).wait_send()

        @pl.when(o < outer - 1)
        def _():
            relay(which, me, UP, src).wait_send()

        @pl.when(o > 0)
        def _():
            relay(which, me, DOWN, src).wait_send()

    for which in (SK, SV):

        @pl.when(o < outer - 1)
        def _():
            relay(which, me, UP).wait_send()

        @pl.when(i == 0)
        def _():
            relay(which, me, ACROSS).wait_send()

    def drain(k, carry):
        low, high = me - 2 * k, me + 2 * k

        @pl.when(o - k >= 0)
        def _():
            for which in (CK, CV, SK, SV):

                @pl.when(o < outer - 1)
                def _():
                    relay(which, low, UP).wait_send()

                @pl.when((which != CV) | (o != k))
                def _():
                    relay(which, low, ACROSS).wait_send()

        @pl.when(o + k < outer)
        def _():
            for which in (CK, CV):

                @pl.when(o > 0)
                def _():
                    relay(which, high, DOWN).wait_send()

                @pl.when((which != CV) | (o + k != outer - 1))
                def _():
                    relay(which, high, ACROSS).wait_send()

        return carry

    lend(lambda copy: copy.wait_send())

    @pl.when((o > 0) & (o < outer - 1))
    def _():
        relay(CV, lent_low, UP).wait_send()
        relay(CV, lent_high, DOWN).wait_send()

    lax.fori_loop(1, outer, drain, 0)


def solution(mesh):
    layers, n = mesh.shape["section"], mesh.shape["seq"]

    def per_device(queries, keys, values, cache_keys, cache_values, vertical, count, slash):
        tok, wide = queries.shape[1:]
        kv_wide = keys.shape[2]
        part = cache_keys.shape[2]
        per = tok // BLK
        dtype = queries.dtype
        rows = n * tok
        anywhere = pl.BlockSpec(memory_space=pltpu.HBM)
        scalars = pl.BlockSpec(memory_space=pltpu.SMEM)
        keys_all = GROUP * part + n * tok
        result = pl.pallas_call(
            functools.partial(kernel, layers, n),
            out_shape=pltpu.VMEM((tok, wide), dtype),
            in_specs=[anywhere] * 5 + [scalars] * 3,
            out_specs=pl.BlockSpec(memory_space=pltpu.VMEM),
            scratch_shapes=[
                pltpu.VMEM((n, part, HEAD), dtype),
                pltpu.VMEM((n, part, HEAD), dtype),
                pltpu.VMEM((n, tok, kv_wide), dtype),
                pltpu.VMEM((n, tok, kv_wide), dtype),
                pltpu.VMEM((tok, wide), dtype),
                pltpu.VMEM((n * per, 1, LANES), jnp.float32),
                pltpu.VMEM((n, per, 1, LANES), jnp.float32),
                pltpu.VMEM((rows, 2 * HEAD), dtype),
                pltpu.VMEM((rows, 2 * HEAD), jnp.float32),
                pltpu.VMEM((rows, LANES), jnp.float32),
                pltpu.SemaphoreType.DMA((2,)),
                pltpu.SemaphoreType.DMA((3,)),
                pltpu.SemaphoreType.DMA,
                pltpu.SemaphoreType.DMA((3, 4, n)),
                pltpu.SemaphoreType.DMA((4, n)),
                pltpu.SemaphoreType.DMA((n,)),
                pltpu.SemaphoreType.DMA((n,)),
            ],
            compiler_params=pltpu.CompilerParams(
                collective_id=0, has_side_effects=True, vmem_limit_bytes=60 * 2**20
            ),
            cost_estimate=pl.CostEstimate(
                flops=4 * rows * keys_all * HEAD,
                bytes_accessed=2 * rows * HEAD * 4,
                transcendentals=rows * keys_all,
            ),
        )(
            queries[0],
            keys[0],
            values[0],
            cache_keys[0, 0],
            cache_values[0, 0],
            vertical[0],
            count,
            slash[0],
        )
        return result[None]

    return jax.shard_map(
        per_device,
        mesh=mesh,
        in_specs=(
            P("section", "seq", None),
            P("section", "seq", None),
            P("section", "seq", None),
            P("section", "seq", None, None),
            P("section", "seq", None, None),
            P("section", "seq", None),
            P("section", "seq"),
            P("section", "seq", None),
        ),
        out_specs=P("section", "seq", None),
        check_vma=False,
    )
```

```python
import functools
import math

import jax
import jax.numpy as jnp
from jax import lax
from jax.experimental import pallas as pl
from jax.experimental.pallas import tpu as pltpu
from jax.sharding import PartitionSpec as P

HEAD = 128
GROUP = 8
BLK = 64
NVMAX = 32
NS = 11
LANES = 128
MASKED = -1e30
MESH = pl.DeviceIdType.MESH
UP, DOWN, ACROSS = 0, 1, 2
CK, CV, SK, SV = 0, 1, 2, 3


def kernel(
    layers,
    n,
    q_hbm,
    k_hbm,
    v_hbm,
    ck_hbm,
    cv_hbm,
    vert_ref,
    count_ref,
    slash_ref,
    out_ref,
    ckbuf,
    cvbuf,
    skbuf,
    svbuf,
    qbuf,
    tabs,
    tabr,
    qaug,
    acc,
    top,
    local_sem,
    shift_send,
    q_recv,
    send_sem,
    recv_sem,
    tab_send,
    tab_recv,
):
    tok = qbuf.shape[0]
    part = ckbuf.shape[1]
    kvh = skbuf.shape[2] // HEAD
    per = tok // BLK
    ncb = GROUP * part // BLK
    nqb = n * per
    rows_of_group = GROUP * tok
    tile = min(2 * tok, rows_of_group)
    outer = n // 2
    sec = lax.axis_index("section")
    me = lax.axis_index("seq")
    o, i = me // 2, me % 2
    after, before = lax.rem(sec + 1, layers), lax.rem(sec + layers - 1, layers)
    scale = math.log2(math.e) / math.sqrt(HEAD)

    barrier = pltpu.get_barrier_semaphore()
    for d in range(1, n):
        pl.semaphore_signal(
            barrier, inc=1, device_id={"seq": lax.rem(me + d, n)}, device_id_type=MESH
        )
    for other in (after, before):
        pl.semaphore_signal(barrier, inc=1, device_id={"section": other}, device_id_type=MESH)
    pl.semaphore_wait(barrier, n + 1)

    bufs = (ckbuf, cvbuf, skbuf, svbuf)
    target = (me + 2, me - 2, me + 1 - 2 * i)

    def relay(which, slot, way, src=None):
        dst = bufs[which].at[slot]
        return pltpu.make_async_remote_copy(
            src_ref=dst if src is None else src,
            dst_ref=dst,
            send_sem=send_sem.at[way, which, slot],
            recv_sem=recv_sem.at[which, slot],
            device_id={"seq": target[way]},
            device_id_type=MESH,
        )

    def shift(src, dst, index, recv):
        return pltpu.make_async_remote_copy(
            src_ref=src,
            dst_ref=dst,
            send_sem=shift_send.at[index],
            recv_sem=recv,
            device_id={"section": after},
            device_id_type=MESH,
        )

    shifts = (
        shift(k_hbm, skbuf.at[me], 0, recv_sem.at[SK, me]),
        shift(v_hbm, svbuf.at[me], 1, recv_sem.at[SV, me]),
        shift(q_hbm, qbuf, 2, q_recv),
    )
    for copy in shifts:
        copy.start()
    own = ((CK, ck_hbm), (CV, cv_hbm))
    for which, src in own:
        relay(which, me, ACROSS, src).start()

        @pl.when(o < outer - 1)
        def _():
            relay(which, me, UP, src).start()

        @pl.when(o > 0)
        def _():
            relay(which, me, DOWN, src).start()

    locals_ = [
        pltpu.make_async_copy(src, bufs[which].at[me], local_sem.at[which]) for which, src in own
    ]
    for copy in locals_:
        copy.start()

    lane = lax.broadcasted_iota(jnp.int32, (1, LANES), 1)
    count = count_ref[0, 0]
    hit = lane < 0
    for slot in range(NVMAX):
        hit = hit | (lane == jnp.where(slot < count, vert_ref[0, slot], -1))
    listed = jnp.where(hit, 1, 0)
    offsets = [slash_ref[0, j] for j in range(NS)]

    def fill(b, carry):
        diagonal = ncb + b
        found = (listed > 0) | (lane == diagonal)
        for off in offsets:
            found = found | (lane == diagonal - off)
        tabs[b] = jnp.where(found, 0.0, MASKED)
        return carry

    lax.fori_loop(0, nqb, fill, 0)

    def table(d):
        to = lax.rem(me + d, n)
        return pltpu.make_async_remote_copy(
            src_ref=tabs.at[pl.ds(to * per, per)],
            dst_ref=tabr.at[me],
            send_sem=tab_send.at[d],
            recv_sem=tab_recv.at[me],
            device_id={"seq": to},
            device_id_type=MESH,
        )

    for d in range(1, n):
        table(d).start()
    tabr[me] = tabs[pl.ds(me * per, per)]

    for which in (SK, SV):
        relay(which, me, UP).wait_recv()

        @pl.when(o < outer - 1)
        def _():
            relay(which, me, UP).start()

        @pl.when(i == 0)
        def _():
            relay(which, me, ACROSS).start()

    def attend(keys, values, first_block, base, diagonal=False):
        width = keys.shape[0]
        block = lax.broadcasted_iota(jnp.int32, (width, LANES), 0) // BLK + first_block
        mark = lax.broadcasted_iota(jnp.int32, (width, LANES), 1) == block
        keys = jnp.concatenate([keys, jnp.where(mark, 1.0, 0.0).astype(jnp.bfloat16)], axis=1)
        values = jnp.concatenate([values, jnp.ones((width, LANES), jnp.bfloat16)], axis=1)
        span = width // LANES

        def scores_of(rows):
            scores = lax.dot_general(
                qaug[rows, :], keys, (((1,), (1,)), ((), ())), preferred_element_type=jnp.float32
            )
            if diagonal:
                token = lax.rem(lax.broadcasted_iota(jnp.int32, (tile, width), 0), tok)
                key = lax.broadcasted_iota(jnp.int32, (tile, width), 1)
                scores = jnp.where(key <= token, scores, MASKED)
            return scores

        def update(rows, scores):
            high = jnp.broadcast_to(jnp.max(scores, axis=1, keepdims=True), (tile, LANES))
            if not diagonal:
                old = top[rows, :]
                high = jnp.maximum(old, high)
            top[rows, :] = high
            wide = jnp.concatenate([high] * span, axis=1)
            weights = jnp.exp2((scores - wide) * scale).astype(jnp.bfloat16)
            fresh = jnp.dot(weights, values, preferred_element_type=jnp.float32)
            if diagonal:
                acc[rows, :] = fresh
            else:
                factor = jnp.exp2((old - high) * scale)
                acc[rows, :] = acc[rows, :] * jnp.concatenate([factor] * 2, axis=1) + fresh

        spans = [
            pl.ds(base + t * tile if kvh == 1 else pl.multiple_of(base + t * tile, tile), tile)
            for t in range(rows_of_group // tile)
        ]
        ahead = scores_of(spans[0])
        for t, rows in enumerate(spans):
            scores = ahead
            if t + 1 < len(spans):
                ahead = scores_of(spans[t + 1])
            update(rows, scores)

    def attend_cache(slot):
        attend(
            ckbuf[slot],
            cvbuf[slot],
            lax.rem(slot, GROUP) * (part // BLK),
            0 if kvh == 1 else slot // GROUP * rows_of_group,
        )

    def attend_stretch(slot, slots, diagonal=False):
        for g in range(kvh):
            keys = skbuf[pl.ds(slot, slots), :, g * HEAD : (g + 1) * HEAD]
            values = svbuf[pl.ds(slot, slots), :, g * HEAD : (g + 1) * HEAD]
            attend(
                keys.reshape(slots * tok, HEAD),
                values.reshape(slots * tok, HEAD),
                ncb + slot * per,
                g * rows_of_group,
                diagonal,
            )

    def across(k):
        low, high = me - 2 * k + 1 - 2 * i, me + 2 * k + 1 - 2 * i

        @pl.when(o - k >= 0)
        def _():
            for which in (SK, SV):
                relay(which, low, ACROSS).wait_recv()
            attend_stretch((o - k) * 2, 2)
            relay(CK, low, ACROSS).wait_recv()

            @pl.when(o != k)
            def _():
                relay(CV, low, ACROSS).wait_recv()

            attend_cache(low)

        @pl.when(o + k < outer)
        def _():
            relay(CK, high, ACROSS).wait_recv()

            @pl.when(o + k != outer - 1)
            def _():
                relay(CV, high, ACROSS).wait_recv()

            attend_cache(high)

    partner = me + 1 - 2 * i
    lent_low, lent_high = 1 - i, 2 * (outer - 1) + 1 - i

    def lend(action):
        @pl.when(o == 0)
        def _():
            action(relay(CV, partner, UP))

        @pl.when(o == outer - 1)
        def _():
            action(relay(CV, partner, DOWN))

    def pass_lent(k):
        @pl.when(o == k)
        def _():
            relay(CV, lent_low, UP).wait_recv()

            @pl.when(o < outer - 1)
            def _():
                relay(CV, lent_low, UP).start()

        @pl.when(o + k == outer - 1)
        def _():
            relay(CV, lent_high, DOWN).wait_recv()

            @pl.when(o > 0)
            def _():
                relay(CV, lent_high, DOWN).start()

    def pass_up(k, *arrays):
        low = me - 2 * k

        @pl.when(o - k >= 0)
        def _():
            for which in arrays:
                relay(which, low, UP).wait_recv()

                @pl.when(o < outer - 1)
                def _():
                    relay(which, low, UP).start()

                @pl.when((which != CV) | (o != k))
                def _():
                    relay(which, low, ACROSS).start()

    def pass_down(k, *arrays):
        high = me + 2 * k

        @pl.when(o + k < outer)
        def _():
            for which in arrays:
                relay(which, high, DOWN).wait_recv()

                @pl.when(o > 0)
                def _():
                    relay(which, high, DOWN).start()

                @pl.when((which != CV) | (o + k != outer - 1))
                def _():
                    relay(which, high, ACROSS).start()

    def along(k):
        @pl.when(o - k >= 0)
        def _():
            attend_cache(me - 2 * k)

        @pl.when(o + k < outer)
        def _():
            attend_cache(me + 2 * k)

    pass_up(1, CK)
    pass_down(1, CK)
    shifts[2].wait_recv()
    for d in range(1, n):
        src = lax.rem(me + d, n)
        pltpu.make_async_remote_copy(
            src_ref=tabs.at[pl.ds(0, per)],
            dst_ref=tabr.at[src],
            send_sem=tab_send.at[d],
            recv_sem=tab_recv.at[src],
            device_id={"seq": src},
            device_id_type=MESH,
        ).wait_recv()
    for h in range(n):
        qaug[h * tok : (h + 1) * tok, :HEAD] = qbuf[:, h * HEAD : (h + 1) * HEAD]
        for j in range(per):
            qaug[h * tok + j * BLK : h * tok + (j + 1) * BLK, HEAD:] = jnp.broadcast_to(
                tabr[h, j].astype(jnp.bfloat16), (BLK, LANES)
            )

    pass_up(1, CV)
    pass_down(1, CV)
    attend_stretch(me, 1, diagonal=True)
    relay(CV, partner, ACROSS).wait_recv()
    lend(lambda copy: copy.start())
    pass_up(1, SK, SV)
    for copy in locals_:
        copy.wait()
    attend_cache(me)
    relay(CK, partner, ACROSS).wait_recv()
    attend_cache(partner)

    @pl.when(i == 1)
    def _():
        for which in (SK, SV):
            relay(which, partner, ACROSS).wait_recv()
        attend_stretch(partner, 1)

    def step(k, carry):
        along(k - 1)
        pass_lent(k - 1)
        pass_up(k, CK)
        pass_down(k, CK)
        pass_up(k, SK, SV)
        pass_up(k, CV)
        pass_down(k, CV)
        across(k - 1)
        return carry

    lax.fori_loop(2, outer, step, 0)
    along(outer - 1)
    pass_lent(outer - 1)
    across(outer - 1)

    for h in range(n):
        rows = slice(h * tok, (h + 1) * tok)
        out_ref[:, h * HEAD : (h + 1) * HEAD] = (acc[rows, :HEAD] / acc[rows, HEAD:]).astype(
            out_ref.dtype
        )

    for copy in shifts:
        copy.wait_send()
    for d in range(1, n):
        table(d).wait_send()
    for which, src in own:
        relay(which, me, ACROSS, src).wait_send()

        @pl.when(o < outer - 1)
        def _():
            relay(which, me, UP, src).wait_send()

        @pl.when(o > 0)
        def _():
            relay(which, me, DOWN, src).wait_send()

    for which in (SK, SV):

        @pl.when(o < outer - 1)
        def _():
            relay(which, me, UP).wait_send()

        @pl.when(i == 0)
        def _():
            relay(which, me, ACROSS).wait_send()

    def drain(k, carry):
        low, high = me - 2 * k, me + 2 * k

        @pl.when(o - k >= 0)
        def _():
            for which in (CK, CV, SK, SV):

                @pl.when(o < outer - 1)
                def _():
                    relay(which, low, UP).wait_send()

                @pl.when((which != CV) | (o != k))
                def _():
                    relay(which, low, ACROSS).wait_send()

        @pl.when(o + k < outer)
        def _():
            for which in (CK, CV):

                @pl.when(o > 0)
                def _():
                    relay(which, high, DOWN).wait_send()

                @pl.when((which != CV) | (o + k != outer - 1))
                def _():
                    relay(which, high, ACROSS).wait_send()

        return carry

    lend(lambda copy: copy.wait_send())

    @pl.when((o > 0) & (o < outer - 1))
    def _():
        relay(CV, lent_low, UP).wait_send()
        relay(CV, lent_high, DOWN).wait_send()

    lax.fori_loop(1, outer, drain, 0)


def solution(mesh):
    layers, n = mesh.shape["section"], mesh.shape["seq"]

    def per_device(queries, keys, values, cache_keys, cache_values, vertical, count, slash):
        tok, wide = queries.shape[1:]
        kv_wide = keys.shape[2]
        part = cache_keys.shape[2]
        per = tok // BLK
        dtype = queries.dtype
        rows = n * tok
        anywhere = pl.BlockSpec(memory_space=pltpu.HBM)
        scalars = pl.BlockSpec(memory_space=pltpu.SMEM)
        keys_all = GROUP * part + n * tok
        result = pl.pallas_call(
            functools.partial(kernel, layers, n),
            out_shape=pltpu.VMEM((tok, wide), dtype),
            in_specs=[anywhere] * 5 + [scalars] * 3,
            out_specs=pl.BlockSpec(memory_space=pltpu.VMEM),
            scratch_shapes=[
                pltpu.VMEM((n, part, HEAD), dtype),
                pltpu.VMEM((n, part, HEAD), dtype),
                pltpu.VMEM((n, tok, kv_wide), dtype),
                pltpu.VMEM((n, tok, kv_wide), dtype),
                pltpu.VMEM((tok, wide), dtype),
                pltpu.VMEM((n * per, 1, LANES), jnp.float32),
                pltpu.VMEM((n, per, 1, LANES), jnp.float32),
                pltpu.VMEM((rows, 2 * HEAD), dtype),
                pltpu.VMEM((rows, 2 * HEAD), jnp.float32),
                pltpu.VMEM((rows, LANES), jnp.float32),
                pltpu.SemaphoreType.DMA((2,)),
                pltpu.SemaphoreType.DMA((3,)),
                pltpu.SemaphoreType.DMA,
                pltpu.SemaphoreType.DMA((3, 4, n)),
                pltpu.SemaphoreType.DMA((4, n)),
                pltpu.SemaphoreType.DMA((n,)),
                pltpu.SemaphoreType.DMA((n,)),
            ],
            compiler_params=pltpu.CompilerParams(
                collective_id=0, has_side_effects=True, vmem_limit_bytes=60 * 2**20
            ),
            cost_estimate=pl.CostEstimate(
                flops=4 * rows * keys_all * HEAD,
                bytes_accessed=2 * rows * HEAD * 4,
                transcendentals=rows * keys_all,
            ),
        )(
            queries[0],
            keys[0],
            values[0],
            cache_keys[0, 0],
            cache_values[0, 0],
            vertical[0],
            count,
            slash[0],
        )
        return result[None]

    return jax.shard_map(
        per_device,
        mesh=mesh,
        in_specs=(
            P("section", "seq", None),
            P("section", "seq", None),
            P("section", "seq", None),
            P("section", "seq", None, None),
            P("section", "seq", None, None),
            P("section", "seq", None),
            P("section", "seq"),
            P("section", "seq", None),
        ),
        out_specs=P("section", "seq", None),
        check_vma=False,
    )
```
